512 devices in a mesh: blk: 64 (over z_lo, y, core), uly: 8 (over x, z_hi).
Axes of the slice: x: 4, y: 8, z: 8 (z_hi: 2, z_lo: 4; z = z_hi * 4 + z_lo), core: 2. Of those that a mesh axis runs over, the one named last changes fastest.
Arguments:
- query: bfloat16 [8192, 3072], P(('blk', 'uly')), may hold values from -64 to 64
- key: bfloat16 [8192, 3072], P(('blk', 'uly')), may hold values from -64 to 64
- value: bfloat16 [8192, 3072], P(('blk', 'uly')), may hold values from -6 to 6
- tile_list: int32 [64, 32], P('blk'), may hold values from -1 to 63, as said below
Outputs:
- attended: bfloat16 [8192, 3072], P(('blk', 'uly'))
The draws below stay inside these ranges and needn't reach their ends.
Inputs may be any that keep to these rules, and one draw needn't show every extreme that they name: `tile_list`: each row lists distinct key tiles, its own tile among them, followed by -1 in unused slots; at least 2 slots are used and some row uses all 32.
All inputs are finite; a program needn't handle non-finite values.
Results may differ from the reference program's by a relative error of at most 0.0085.
Values may be sent and summed in bfloat16 or wider, within the bound.
A program may use at most 64 MiB of HBM per device.

```python
import jax
import jax.numpy as jnp
from jax import lax

HEAD_DIM = 128
HEADS = 24
TILE = 128
TOKENS = 8192
KTILES = 64
MAXT = 32


def shared_rows(key):
    return jnp.clip(jax.random.normal(key, (TOKENS, HEADS * HEAD_DIM), jnp.float32), -4.0, 4.0)


def draw_key(key, part):
    common = shared_rows(key)
    return common.astype(jnp.bfloat16)


def draw_query(key, part):
    key = jax.random.fold_in(key, 11)
    own_rows = jnp.clip(jax.random.normal(key, (TOKENS, HEADS * HEAD_DIM), jnp.float32), -6.0, 6.0)
    return own_rows.astype(jnp.bfloat16)


def draw_tile_list(key, part):
    key = jax.random.fold_in(key, 3)
    key_noise, key_counts, key_full = jax.random.split(key, 3)
    tile_ids = jnp.arange(KTILES, dtype=jnp.int32)
    noise = jax.random.randint(key_noise, (KTILES, KTILES), 0, 2 * KTILES)
    distance = jnp.abs(tile_ids[:, None] - tile_ids[None, :])
    score = noise - distance + jnp.where(distance == 0, 8 * KTILES, 0)
    ranked = (score + 2 * KTILES) * KTILES + tile_ids[None, :]
    ranked_values, order = lax.top_k(ranked, MAXT)
    counts = jax.random.randint(key_counts, (KTILES,), 2, MAXT + 1)
    full_row = jax.random.randint(key_full, (), 0, KTILES)
    counts = jnp.where(tile_ids == full_row, MAXT, counts)
    slots = jnp.arange(MAXT, dtype=jnp.int32)
    return jnp.where(slots[None, :] < counts[:, None], order.astype(jnp.int32), -1).astype(jnp.int32)


def level_of(own_key, dims, cuts, least, top_value):
    factor_of = 1.0
    for position, blocks in cuts:
        heights = jax.random.uniform(jax.random.fold_in(jax.random.fold_in(own_key, 6), position), (blocks,), jnp.float32, least / len(cuts), top_value / len(cuts))
        factor_of = factor_of * jnp.repeat(jnp.exp(heights), dims[position] // blocks).reshape((-1,) + (1,) * (len(dims) - 1 - position))
    return factor_of


def scatter_about(key, dims, deviation, bound, cuts=(), kind=jnp.bfloat16):
    values = deviation * jax.random.normal(key, dims, jnp.float32)
    if cuts:
        values = values * level_of(key, dims, cuts, -0.22, 0.18)
    return jnp.clip(values, -bound, bound).astype(kind)


def setup_inputs(seed: int = 0) -> dict:
    streams_of = jax.random.split(jax.random.key(seed), 5)
    query = draw_query(jax.random.fold_in(streams_of[4], 71), 0)
    key = draw_key(jax.random.fold_in(streams_of[4], 71), 0)
    value = scatter_about(streams_of[2], (TOKENS, HEADS * HEAD_DIM), 1.0, 6.0, ((0, 512),))
    tile_list = draw_tile_list(jax.random.fold_in(streams_of[4], 71), 0)
    return {"query": query, "key": key, "value": value, "tile_list": tile_list}


def reference(query, key, value, tile_list):
    scale = HEAD_DIM ** -0.5
    query_all = query.reshape(TOKENS, HEADS, HEAD_DIM)
    key_float = key.reshape(TOKENS, HEADS, HEAD_DIM).astype(jnp.float32)
    value_float = value.reshape(TOKENS, HEADS, HEAD_DIM).astype(jnp.float32)
    tile_ids = jnp.arange(KTILES, dtype=jnp.int32)
    allowed_tiles = jnp.any(tile_list[:, :, None] == tile_ids[None, None, :], axis=1)

    def one_tile(tile_index):
        query_tile = lax.dynamic_slice_in_dim(query_all, tile_index * TILE, TILE, 0).astype(jnp.float32)
        scores = jnp.einsum("qhd,khd->hqk", query_tile, key_float) * scale
        allowed = jnp.repeat(allowed_tiles[tile_index], TILE)[None, None, :]
        scores = jnp.where(allowed, scores, -jnp.inf)
        highest = jnp.max(scores, axis=-1, keepdims=True)
        expo = jnp.exp(scores - highest)
        denominator = jnp.sum(expo, axis=-1)
        weights = expo.astype(jnp.bfloat16).astype(jnp.float32)
        numerator = jnp.einsum("hqk,khd->qhd", weights, value_float)
        result = numerator / jnp.transpose(denominator)[:, :, None]
        return result.astype(jnp.bfloat16).reshape(TILE, HEADS * HEAD_DIM)

    tiles = lax.map(one_tile, jnp.arange(KTILES, dtype=jnp.int32))
    return tiles.reshape(TOKENS, HEADS * HEAD_DIM)
```

```python
import jax
import jax.numpy as jnp
from jax import lax
from jax.experimental import pallas as pl
from jax.experimental.pallas import tpu as pltpu
from jax.sharding import PartitionSpec as P

MESH = pl.DeviceIdType.MESH
D = 128
HEADS = 24
NX, NYH, NZ = 4, 4, 8
ROWS = 16
SRC = NYH * NZ
GROUP = SRC * ROWS
QTILES = 16
SLOTS = 32
PART = 32
CHUNKS = 4
PER_CHUNK = QTILES // CHUNKS
SCALE = 1.4426950408889634 / 128**0.5
LOW = -1e30
F32, BF16 = jnp.float32, jnp.bfloat16


def kernel(
    q_hbm, k_hbm, v_hbm, list_ref, out_ref,
    qin, kvin, list_src, lists, used, places, places_s, kv, qs, part, got, stat, got_stat, fin,
    in_sem, self_sem, a_send, a_recv, kv_send, kv_recv, q_send, q_recv, d_send, d_recv, s_send, s_recv, e_sem, e_self,
):
    blk, uly = lax.axis_index("blk"), lax.axis_index("uly")
    c, y, zl = blk % 2, (blk // 2) % 8, blk // 16
    x, zh = uly // 2, uly % 2
    yh, yl = y // 2, y % 2
    z = zh * 4 + zl
    active = yh < 3

    def device(x, yh, yl, z, c):
        return (((z % 4) * 8 + yh * 2 + yl) * 2 + c, x * 2 + z // 4)

    def slot(yh, z):
        return ((z % 4) * 4 + yh) * 2 + z // 4

    loads = [
        pltpu.make_async_copy(k_hbm, kvin.at[0], in_sem.at[0]),
        pltpu.make_async_copy(v_hbm, kvin.at[1], in_sem.at[1]),
        pltpu.make_async_copy(q_hbm, qin, in_sem.at[2]),
    ]
    for load in loads:
        load.start()

    barrier = pltpu.get_barrier_semaphore()

    def greet(i, carry):
        tyh, tz = (yh + i // NZ) % NYH, (z + i) % NZ

        @pl.when(jnp.logical_or(active, tyh < 3))
        def _():
            pl.semaphore_signal(barrier, inc=1, device_id=device(x, tyh, yl, tz, c), device_id_type=MESH)

        return carry

    lax.fori_loop(1, SRC, greet, 0)
    chip_peer = device(x, yh, yl, z, 1 - c)
    y_peer = device(x, yh, 1 - yl, z, c)
    x_peers = [device((x + r) % NX, yh, yl, z, c) for r in range(1, NX)]

    @pl.when(active)
    def _():
        for peer in (chip_peer, y_peer, *x_peers):
            pl.semaphore_signal(barrier, inc=1, device_id=peer, device_id_type=MESH)

    list_src[...] = jnp.full_like(list_src, -1)
    list_src[:, 0:SLOTS] = list_ref[...]
    stat[...] = jnp.zeros_like(stat)

    @pl.when(active)
    def _():
        pl.semaphore_wait(barrier, SRC - 1 + 5)

    @pl.when(jnp.logical_not(active))
    def _():
        pl.semaphore_wait(barrier, HEADS)

    mine = slot(yh, z)
    own = yl * 2 + c

    def kv_cols(h):
        return kvin.at[:, :, pl.ds(pl.multiple_of(h * D, D), D)]

    def q_cols(h):
        return qin.at[:, pl.ds(pl.multiple_of(h * D, D), D)]

    kv_rows = kv.at[:, own * QTILES + mine // 2, pl.ds(pl.multiple_of(mine % 2 * ROWS, ROWS), ROWS), :]
    q_rows = qs.at[x, pl.ds(pl.multiple_of(mine * ROWS, ROWS), ROWS), :]
    list_row = lists.at[mine]

    def target(i):
        tyh, tz = (yh + i % 3) % 3, (z + i // 3) % NZ
        return tz * 3 + tyh, device(x, tyh, yl, tz, c)

    def send_kv(i, carry):
        h, dev = target(i)
        pltpu.make_async_remote_copy(kv_cols(h), kv_rows, a_send.at[0], a_recv.at[0], device_id=dev, device_id_type=MESH).start()
        return carry

    def send_q(i, carry):
        h, dev = target(i)
        pltpu.make_async_remote_copy(q_cols(h), q_rows, a_send.at[1], a_recv.at[1], device_id=dev, device_id_type=MESH).start()
        pltpu.make_async_remote_copy(list_src, list_row, a_send.at[2], a_recv.at[2], device_id=dev, device_id_type=MESH).start()
        return carry

    head = z * 3 + yh
    first = jnp.where(active, 1, 0)
    loads[0].wait()
    loads[1].wait()
    lax.fori_loop(first, HEADS, send_kv, 0)
    loads[2].wait()
    lax.fori_loop(first, HEADS, send_q, 0)

    @pl.when(active)
    def _():
        selves = [
            pltpu.make_async_copy(kv_cols(head), kv_rows, self_sem.at[0]),
            pltpu.make_async_copy(q_cols(head), q_rows, self_sem.at[1]),
            pltpu.make_async_copy(list_src, list_row, self_sem.at[2]),
        ]
        for copy in selves:
            copy.start()

        def kv_copy(i, which, place, dev):
            block = kv.at[which, pl.ds(place * QTILES, QTILES)]
            return pltpu.make_async_remote_copy(block, block, kv_send.at[i], kv_recv.at[i], device_id=dev, device_id_type=MESH)

        far = (1 - yl) * 2 + c
        y_copies = [kv_copy(w, w, own, y_peer) for w in range(2)]
        chip_copies = [kv_copy(2 + w, w, own, chip_peer) for w in range(2)]
        on_copies = [kv_copy(4 + w, w, far, chip_peer) for w in range(2)]
        q_copies = [
            pltpu.make_async_remote_copy(qs.at[x], qs.at[x], q_send.at[r], q_recv.at[r], device_id=x_peers[r], device_id_type=MESH)
            for r in range(NX - 1)
        ]
        n = (SRC - 1) * ROWS
        selves[0].wait()
        arrived = kv.at[0, pl.ds(0, SRC - 1)]
        pltpu.make_async_copy(arrived, arrived, a_recv.at[0]).wait()
        for copy in y_copies:
            copy.start()
        for copy in chip_copies:
            copy.start()
        selves[1].wait()
        arrived = qs.at[0, pl.ds(0, n), :]
        pltpu.make_async_copy(arrived, arrived, a_recv.at[1]).wait()
        for copy in q_copies:
            copy.start()
        selves[2].wait()
        arrived = lists.at[pl.ds(0, SRC - 1)]
        pltpu.make_async_copy(arrived, arrived, a_recv.at[2]).wait()
        listed = lists[...]
        used[...] = jnp.broadcast_to(jnp.sum(jnp.where(listed >= 0, PART, 0), axis=2, keepdims=True), used.shape)
        listed = jnp.maximum(listed, 0)
        places[...] = (listed & 3) * QTILES + (listed >> 2)
        to_scalars = pltpu.make_async_copy(places, places_s, self_sem.at[3])
        to_scalars.start()
        for w in range(2):
            y_copies[w].wait_recv()
            on_copies[w].start()
        to_scalars.wait()
        for copy in q_copies:
            copy.wait_recv()
        for copy in chip_copies + on_copies:
            copy.wait_recv()

        lane = lax.broadcasted_iota(jnp.int32, (D, D), 1)
        key_lane = lax.broadcasted_iota(jnp.int32, (1, 256), 1)
        ones = jnp.ones((256, D), BF16)

        def tile(t):
            query = jnp.concatenate([qs[i, pl.ds(pl.multiple_of(t * PART, PART), PART), :] for i in range(NX)], axis=0)
            blocks = [places_s[2 * t, 0, s] for s in range(SLOTS)]
            limit = used[2 * t]
            limit = jnp.concatenate([limit, limit], axis=1)
            scores = []
            for g in range(4):
                keys = jnp.concatenate([kv[0, b] for b in blocks[g * 8 : g * 8 + 8]], axis=0)
                s = lax.dot_general(query, keys, (((1,), (1,)), ((), ())), preferred_element_type=F32)
                scores.append(s + jnp.where(key_lane < limit - g * 256, 0.0, LOW))
            top = jnp.maximum(jnp.maximum(scores[0], scores[1]), jnp.maximum(scores[2], scores[3]))
            top = jnp.max(top, axis=1, keepdims=True)
            total = jnp.zeros((D, 2 * D), F32)
            for g in range(4):
                weights = jnp.exp2((scores[g] - top) * SCALE).astype(BF16)
                values = jnp.concatenate([kv[1, b] for b in blocks[g * 8 : g * 8 + 8]], axis=0)
                total = total + jnp.dot(weights, jnp.concatenate([values, ones], axis=1), preferred_element_type=F32)
            stat[...] = jnp.where(lane == t, top, jnp.where(lane == t + 64, total[:, D:], stat[...]))
            numerator = total[:, :D].astype(BF16)
            for i in range(NX):
                part[(i - x + NX) % NX, pl.ds(pl.multiple_of(t * PART, PART), PART), :] = numerator[i * PART : (i + 1) * PART]

        def part_copy(k, r):
            rows = pl.ds(pl.multiple_of(k * (PER_CHUNK * PART), PER_CHUNK * PART), PER_CHUNK * PART)
            return pltpu.make_async_remote_copy(
                part.at[r, rows, :], got.at[r - 1, rows, :], d_send.at[k, r - 1], d_recv.at[k, r - 1],
                device_id=x_peers[r - 1], device_id_type=MESH,
            )

        def chunk(k, carry):
            lax.fori_loop(0, PER_CHUNK, lambda i, n: (tile(k * PER_CHUNK + i), n)[1], 0)
            for r in range(1, NX):
                part_copy(k, r).start()
            return carry

        lax.fori_loop(0, CHUNKS, chunk, 0)
        stat_copies = [
            pltpu.make_async_remote_copy(
                stat.at[pl.ds(pl.multiple_of(((x + r) % NX) * PART, PART), PART), :], got_stat.at[r - 1],
                s_send.at[r - 1], s_recv.at[r - 1], device_id=x_peers[r - 1], device_id_type=MESH,
            )
            for r in range(1, NX)
        ]
        for copy in stat_copies:
            copy.start()

        for copy in stat_copies:
            copy.wait_recv()
        stats = [stat[pl.ds(pl.multiple_of(x * PART, PART), PART), :]] + [got_stat[r] for r in range(NX - 1)]
        highest = jnp.maximum(jnp.maximum(stats[0], stats[1]), jnp.maximum(stats[2], stats[3]))
        factors = [jnp.exp2((s - highest) * SCALE) for s in stats]
        denominator = sum(f[:, 0:QTILES] * s[:, 64 : 64 + QTILES] for f, s in zip(factors, stats))
        factors = [f[:, 0:QTILES] / denominator for f in factors]
        for k in range(CHUNKS):
            for r in range(1, NX):
                part_copy(k, r).wait_recv()
            for t in range(k * PER_CHUNK, (k + 1) * PER_CHUNK):
                rows = slice(t * PART, (t + 1) * PART)
                terms = [part[0, rows, :]] + [got[r, rows, :] for r in range(NX - 1)]
                fin[rows, :] = sum(f[:, t : t + 1] * a.astype(F32) for f, a in zip(factors, terms)).astype(BF16)

        columns = out_ref.at[:, pl.ds(pl.multiple_of(head * D, D), D)]

        def fin_rows(s):
            return fin.at[pl.ds(pl.multiple_of(s * ROWS, ROWS), ROWS), :]

        def send_out(i, carry):
            tyh, tz = (yh + i // NZ) % NYH, (z + i) % NZ
            dev = device(x, tyh, yl, tz, c)
            pltpu.make_async_remote_copy(
                fin_rows(slot(tyh, tz)), columns, e_sem.at[0], e_sem.at[1], device_id=dev, device_id_type=MESH
            ).start()
            return carry

        lax.fori_loop(1, SRC, send_out, 0)
        last = pltpu.make_async_copy(fin_rows(mine), columns, e_self)
        last.start()

        for copy in y_copies + chip_copies + on_copies + q_copies + stat_copies:
            copy.wait_send()
        for k in range(CHUNKS):
            for r in range(1, NX):
                part_copy(k, r).wait_send()
        last.wait()
        sent = fin.at[pl.ds(0, n), :]
        pltpu.make_async_copy(sent, sent, e_sem.at[0]).wait()

    def finish(count):
        cols = pl.ds(0, count * D)
        for ref, sem in (
            (kvin.at[:, :, cols], a_send.at[0]),
            (qin.at[:, cols], a_send.at[1]),
            (lists.at[pl.ds(0, count)], a_send.at[2]),
            (out_ref.at[:, cols], e_sem.at[1]),
        ):
            pltpu.make_async_copy(ref, ref, sem).wait()

    @pl.when(active)
    def _():
        finish(HEADS - 1)

    @pl.when(jnp.logical_not(active))
    def _():
        finish(HEADS)


def per_device(query, key, value, tile_list):
    dma = pltpu.SemaphoreType.DMA
    return pl.pallas_call(
        kernel,
        out_shape=jax.ShapeDtypeStruct(query.shape, BF16),
        in_specs=[pl.BlockSpec(memory_space=pl.ANY)] * 3 + [pl.BlockSpec(memory_space=pltpu.VMEM)],
        out_specs=pl.BlockSpec(memory_space=pl.ANY),
        scratch_shapes=[
            pltpu.VMEM((ROWS, HEADS * D), BF16),
            pltpu.VMEM((2, ROWS, HEADS * D), BF16),
            pltpu.VMEM((1, D), jnp.int32),
            pltpu.VMEM((SRC, 1, D), jnp.int32),
            pltpu.VMEM((SRC, 1, D), jnp.int32),
            pltpu.VMEM((SRC, 1, D), jnp.int32),
            pltpu.SMEM((SRC, 1, D), jnp.int32),
            pltpu.VMEM((2, 4 * QTILES, PART, D), BF16),
            pltpu.VMEM((NX, GROUP, D), BF16),
            pltpu.VMEM((NX, GROUP, D), BF16),
            pltpu.VMEM((NX - 1, GROUP, D), BF16),
            pltpu.VMEM((D, D), F32),
            pltpu.VMEM((NX - 1, PART, D), F32),
            pltpu.VMEM((GROUP, D), BF16),
            dma((3,)), dma((4,)), dma((3,)), dma((3,)), dma((6,)), dma((6,)), dma((3,)), dma((3,)),
            dma((CHUNKS, 3)), dma((CHUNKS, 3)), dma((3,)), dma((3,)), dma((2,)), dma,
        ],
        compiler_params=pltpu.CompilerParams(
            collective_id=0, has_side_effects=True, vmem_limit_bytes=32 * 1024 * 1024
        ),
        name="attention",
    )(query, key, value, tile_list)


def solution(mesh):
    rows = P(("blk", "uly"), None)
    return jax.shard_map(
        per_device,
        mesh=mesh,
        in_specs=(rows, rows, rows, P("blk", None)),
        out_specs=rows,
        check_vma=False,
    )
```

```python
import jax
import jax.numpy as jnp
from jax import lax
from jax.experimental import pallas as pl
from jax.experimental.pallas import tpu as pltpu
from jax.sharding import PartitionSpec as P

MESH = pl.DeviceIdType.MESH
D = 128
HEADS = 24
ROWS = 16
SRC = 32
TILES = 16
HALF = TILES
SLOTS = 32
PART = 32
CHUNKS = 8
PER_CHUNK = 2
SCALE = 1.4426950408889634 / 128**0.5
LOW = -1e30
F32, BF16 = jnp.float32, jnp.bfloat16


def kernel(
    q_hbm, k_hbm, v_hbm, list_ref, out_ref,
    list_src, list_room, lists, used, places, places_s, qkv, part, got, stat, got_stat, fin,
    list_sem, a_send, a_recv, b_send, b_recv, d_send, d_recv, s_send, s_recv, e_sem,
):
    blk, uly = lax.axis_index("blk"), lax.axis_index("uly")
    c, y, x = blk % 2, (blk // 2) % 8, uly // 2
    z = uly % 2 * 4 + blk // 16
    xh, xl, yh, yl, zc, zr = x // 2, x % 2, y // 2, y % 2, z // 2, z % 2
    active = zc < 3

    def device(x, y, z):
        return (((z % 4) * 8 + y) * 2 + c, x * 2 + z // 4)

    def turned(other):
        return jnp.where((other - yh) % 2 == 0, 1 - yl, yl)

    def crossed(other):
        return jnp.where(other == xh, xl, 1 - xl)

    def target(h):
        txh, tyh, tzc = h // 4 % 2, h % 4, h // 8
        zh = z // 4
        return device(2 * txh + crossed(txh), 2 * tyh + turned(tyh), 2 * tzc + jnp.where(tzc == 0, 1 - zh, zh))

    from_z = 4 * jnp.where(zc == 0, 1 - zr, zr)

    def source(s):
        sxh, syh = s // 16, s // 4 % 4
        return device(2 * sxh + crossed(sxh), 2 * syh + turned(syh), from_z + s % 4)

    head = zc * 8 + xh * 4 + yh
    tile = yh * 4 + z % 4
    mine = xh * HALF + tile

    rows_in = (q_hbm, k_hbm, v_hbm)

    def flip(value, by):
        return 1 - value if by else value

    chip_peer = (blk + 1 - 2 * c, uly)
    y_peer = device(x, 2 * yh + 1 - yl, z)
    q_peers = [device(2 * xh + flip(xl, r // 2), y, 2 * zc + flip(zr, r % 2)) for r in range(1, 4)]

    barrier = pltpu.get_barrier_semaphore()

    def greet(dev):
        pl.semaphore_signal(barrier, inc=1, device_id=dev, device_id_type=MESH)

    def loop(low, high, body):
        def step(i, carry):
            body(i)
            return carry

        lax.fori_loop(low, high, step, 0)

    @pl.when(active)
    def _():
        for peer in (chip_peer, y_peer, *q_peers):
            greet(peer)
        loop(0, SRC, lambda s: greet(source(s)))

    list_src[...] = jnp.full_like(list_src, -1)
    list_src[:, 0:SLOTS] = list_ref[...]
    stat[...] = jnp.zeros_like(stat)

    def spread(i, zcs):
        return (zc + i // 8) % zcs * 8 + (xh + i // 4) % 2 * 4 + (yh + i) % 4

    def send(which, h):
        pltpu.make_async_remote_copy(
            rows_in[which].at[:, pl.ds(pl.multiple_of(h * D, D), D)], qkv.at[which, mine], a_send.at[which], a_recv.at[which],
            device_id=target(h), device_id_type=MESH,
        ).start()

    def send_list(h):
        pltpu.make_async_remote_copy(
            list_src, lists.at[tile], a_send.at[3], a_recv.at[3], device_id=target(h), device_id_type=MESH
        ).start()

    @pl.when(active)
    def _():
        pl.semaphore_wait(barrier, HEADS + 5)

    @pl.when(jnp.logical_not(active))
    def _():
        pl.semaphore_wait(barrier, HEADS)

    @pl.when(xh == 0)
    def _():
        loop(0, HEADS, lambda i: send_list(spread(i, 3)))

    for which in range(3):
        loop(0, HEADS, lambda i: send(which, spread(i, 3)))

    def wait_for(ref, sem):
        pltpu.make_async_copy(ref, ref, sem).wait()

    @pl.when(active)
    def _():
        def block(which, place):
            return qkv.at[which, pl.ds(place * SRC, SRC)]

        def swap(which, src, dst, i, dev):
            return pltpu.make_async_remote_copy(
                block(which, src), block(which, dst), b_send.at[which, i], b_recv.at[which, i], device_id=dev, device_id_type=MESH
            )

        q_copies = [swap(0, 0, r, r - 1, q_peers[r - 1]) for r in range(1, 4)]
        y_copies = [None] + [swap(which, 0, 2, 0, y_peer) for which in (1, 2)]
        chip_copies = [None] + [swap(which, 0, 1, 1, chip_peer) for which in (1, 2)]
        on_copies = [None] + [swap(which, 2, 3, 2, chip_peer) for which in (1, 2)]

        wait_for(block(0, 0), a_recv.at[0])
        for copy in q_copies:
            copy.start()

        wait_for(lists, a_recv.at[3])
        listed = lists[...]
        used[...] = jnp.broadcast_to(jnp.sum(jnp.where(listed >= 0, 1, 0), axis=2, keepdims=True), used.shape)
        listed = jnp.maximum(listed, 0)
        tile_yh = (listed >> 2) & 3
        tile_yl = ((listed >> 1) & 1) ^ jnp.where((tile_yh - yh) % 2 == 0, 1, 0)
        place = (tile_yl ^ yl) * 2 + ((listed & 1) ^ c)
        places[...] = place * SRC + tile_yh * 4 + (listed >> 4)
        to_scalars = pltpu.make_async_copy(places, places_s, list_sem)
        to_scalars.start()

        for which in (1, 2):
            wait_for(block(which, 0), a_recv.at[which])
            y_copies[which].start()
            chip_copies[which].start()
        y_copies[1].wait_recv()
        on_copies[1].start()
        to_scalars.wait()
        for copy in q_copies + [chip_copies[1], on_copies[1]]:
            copy.wait_recv()

        y_copies[2].wait_recv()
        on_copies[2].start()
        for copy in (chip_copies[2], on_copies[2]):
            copy.wait_recv()

        lane = lax.broadcasted_iota(jnp.int32, (D, D), 1)
        key_slot = lax.broadcasted_iota(jnp.int32, (1, 256), 1) % D // ROWS
        ones = jnp.ones((256, D), BF16)

        def tiles(ts):
            blocks = [[places_s[t, 0, s] for s in range(SLOTS)] for t in ts]
            limits = [jnp.concatenate([used[t], used[t]], axis=1) for t in ts]

            def gathered(which, blocks, g):
                return jnp.concatenate(
                    [qkv[which, b + half * HALF] for half in range(2) for b in blocks[g * 8 : g * 8 + 8]], axis=0
                )

            scores = []
            for t, b, limit in zip(ts, blocks, limits):
                query = jnp.concatenate([qkv[0, r * SRC + half * HALF + t] for r in range(4) for half in range(2)], axis=0)
                scores.append([
                    lax.dot_general(query, gathered(1, b, g), (((1,), (1,)), ((), ())), preferred_element_type=F32)
                    + jnp.where(key_slot + g * 8 < limit, 0.0, LOW)
                    for g in range(4)
                ])
            tops = []
            for s in scores:
                top = jnp.maximum(jnp.maximum(s[0], s[1]), jnp.maximum(s[2], s[3]))
                tops.append(jnp.max(top, axis=1, keepdims=True))
            totals = []
            for b, s, top in zip(blocks, scores, tops):
                total = jnp.zeros((D, 2 * D), F32)
                for g in range(4):
                    weights = jnp.exp2((s[g] - top) * SCALE).astype(BF16)
                    values = jnp.concatenate([gathered(2, b, g), ones], axis=1)
                    total = total + jnp.dot(weights, values, preferred_element_type=F32)
                totals.append(total)
            stats = stat[...]
            for t, top, total in zip(ts, tops, totals):
                stats = jnp.where(lane == t, top, jnp.where(lane == t + 64, total[:, D:], stats))
                numerator = total[:, :D].astype(BF16)
                for r in range(4):
                    for half in range(2):
                        low = r * PART + half * ROWS
                        part[r, half, t] = numerator[low : low + ROWS]
            stat[...] = stats

        def part_copy(k, r):
            rows = pl.ds(k * PER_CHUNK, PER_CHUNK)
            return pltpu.make_async_remote_copy(
                part.at[r, :, rows], got.at[r - 1, :, rows], d_send.at[k, r - 1], d_recv.at[k, r - 1],
                device_id=q_peers[r - 1], device_id_type=MESH,
            )

        def chunk(k):
            loop(0, PER_CHUNK // 2, lambda i: tiles([k * PER_CHUNK + 2 * i, k * PER_CHUNK + 2 * i + 1]))
            for r in range(1, 4):
                part_copy(k, r).start()

        loop(0, CHUNKS, chunk)
        stat_copies = [
            pltpu.make_async_remote_copy(
                stat.at[pl.ds(r * PART, PART), :], got_stat.at[r - 1], s_send.at[r - 1], s_recv.at[r - 1],
                device_id=q_peers[r - 1], device_id_type=MESH,
            )
            for r in range(1, 4)
        ]
        for copy in stat_copies:
            copy.start()

        for copy in stat_copies:
            copy.wait_recv()
        stats = [stat[0:PART, :]] + [got_stat[r] for r in range(3)]
        highest = jnp.maximum(jnp.maximum(stats[0], stats[1]), jnp.maximum(stats[2], stats[3]))
        factors = [jnp.exp2((s - highest) * SCALE) for s in stats]
        denominator = sum(f[:, 0:TILES] * s[:, 64 : 64 + TILES] for f, s in zip(factors, stats))
        factors = [f[:, 0:TILES] / denominator for f in factors]
        for k in range(CHUNKS):
            for r in range(1, 4):
                part_copy(k, r).wait_recv()
            for t in range(k * PER_CHUNK, (k + 1) * PER_CHUNK):
                for half in range(2):
                    rows = slice(half * ROWS, (half + 1) * ROWS)
                    terms = [part[0, half, t]] + [got[r, half, t] for r in range(3)]
                    fin[half * HALF + t] = sum(f[rows, t : t + 1] * a.astype(F32) for f, a in zip(factors, terms)).astype(BF16)

        columns = out_ref.at[:, pl.ds(pl.multiple_of(head * D, D), D)]

        def send_out(i):
            s = (xh + i // 16) % 2 * HALF + (yh + i // 4) % 4 * 4 + (z + i) % 4
            pltpu.make_async_remote_copy(
                fin.at[s], columns, e_sem.at[0], e_sem.at[1], device_id=source(s), device_id_type=MESH
            ).start()

        loop(0, SRC, send_out)

        for copy in q_copies + y_copies[1:] + chip_copies[1:] + on_copies[1:] + stat_copies:
            copy.wait_send()
        for k in range(CHUNKS):
            for r in range(1, 4):
                part_copy(k, r).wait_send()
        wait_for(fin, e_sem.at[0])

    for which in range(3):
        wait_for(rows_in[which], a_send.at[which])
    wait_for(out_ref, e_sem.at[1])

    @pl.when(xh == 0)
    def _():
        wait_for(list_room, a_send.at[3])


def per_device(query, key, value, tile_list):
    dma = pltpu.SemaphoreType.DMA
    return pl.pallas_call(
        kernel,
        out_shape=jax.ShapeDtypeStruct(query.shape, BF16),
        in_specs=[pl.BlockSpec(memory_space=pltpu.HBM)] * 3 + [pl.BlockSpec(memory_space=pltpu.VMEM)],
        out_specs=pl.BlockSpec(memory_space=pl.ANY),
        scratch_shapes=[
            pltpu.VMEM((1, D), jnp.int32),
            pltpu.VMEM((HEADS, 1, D), jnp.int32),
            pltpu.VMEM((TILES, 1, D), jnp.int32),
            pltpu.VMEM((TILES, 1, D), jnp.int32),
            pltpu.VMEM((TILES, 1, D), jnp.int32),
            pltpu.SMEM((TILES, 1, D), jnp.int32),
            pltpu.VMEM((3, 4 * SRC, ROWS, D), BF16),
            pltpu.VMEM((4, 2, TILES, ROWS, D), BF16),
            pltpu.VMEM((3, 2, TILES, ROWS, D), BF16),
            pltpu.VMEM((D, D), F32),
            pltpu.VMEM((3, PART, D), F32),
            pltpu.VMEM((SRC, ROWS, D), BF16),
            dma, dma((4,)), dma((4,)), dma((3, 3)), dma((3, 3)),
            dma((CHUNKS, 3)), dma((CHUNKS, 3)), dma((3,)), dma((3,)), dma((2,)),
        ],
        compiler_params=pltpu.CompilerParams(
            collective_id=0, has_side_effects=True, vmem_limit_bytes=56 * 1024 * 1024
        ),
        name="attention",
    )(query, key, value, tile_list)


def solution(mesh):
    rows = P(("blk", "uly"), None)
    return jax.shard_map(
        per_device,
        mesh=mesh,
        in_specs=(rows, rows, rows, P("blk", None)),
        out_specs=rows,
        check_vma=False,
    )
```

```python
import jax
import jax.numpy as jnp
from jax import lax
from jax.experimental import pallas as pl
from jax.experimental.pallas import tpu as pltpu
from jax.sharding import PartitionSpec as P

MESH = pl.DeviceIdType.MESH
D = 128
HEADS = 24
ROWS = 16
SRC = 32
TILES = 16
HALF = TILES
SLOTS = 32
PART = 32
CHUNKS = 8
EARLY = 4
PER_CHUNK = 2
SCALE = 1.4426950408889634 / 128**0.5
LOW = -1e30
F32, BF16 = jnp.float32, jnp.bfloat16


def kernel(
    q_hbm, k_hbm, v_hbm, list_ref, out_ref,
    list_src, list_room, lists, used, places, places_s, q_rows, k_rows, v_rows, kept, part, got, stat, got_stat, fin,
    list_sem, a_send, a_recv, b_send, b_recv, d_send, d_recv, s_send, s_recv, e_sem,
):
    blk, uly = lax.axis_index("blk"), lax.axis_index("uly")
    c, y, x = blk % 2, (blk // 2) % 8, uly // 2
    z = uly % 2 * 4 + blk // 16
    xh, xl, yh, yl, zc, zr = x // 2, x % 2, y // 2, y % 2, z // 2, z % 2
    active = zc < 3

    def device(x, y, z):
        return (((z % 4) * 8 + y) * 2 + c, x * 2 + z // 4)

    def turned(other):
        return jnp.where((other - yh) % 2 == 0, 1 - yl, yl)

    def crossed(other):
        return jnp.where(other == xh, xl, 1 - xl)

    def target(h):
        txh, tyh, tzc = h // 4 % 2, h % 4, h // 8
        zh = z // 4
        return device(2 * txh + crossed(txh), 2 * tyh + turned(tyh), 2 * tzc + jnp.where(tzc == 0, 1 - zh, zh))

    from_z = 4 * jnp.where(zc == 0, 1 - zr, zr)

    def source(s):
        sxh, syh = s // 16, s // 4 % 4
        return device(2 * sxh + crossed(sxh), 2 * syh + turned(syh), from_z + s % 4)

    head = zc * 8 + xh * 4 + yh
    tile = yh * 4 + z % 4
    mine = xh * HALF + tile

    rows_in = (q_hbm, k_hbm, v_hbm)
    held = (q_rows, k_rows, v_rows)

    def flip(value, by):
        return 1 - value if by else value

    chip_peer = (blk + 1 - 2 * c, uly)
    y_peer = device(x, 2 * yh + 1 - yl, z)
    q_peers = [device(2 * xh + flip(xl, r // 2), y, 2 * zc + flip(zr, r % 2)) for r in range(1, 4)]

    barrier = pltpu.get_barrier_semaphore()

    def greet(dev):
        pl.semaphore_signal(barrier, inc=1, device_id=dev, device_id_type=MESH)

    def loop(low, high, body):
        def step(i, carry):
            body(i)
            return carry

        lax.fori_loop(low, high, step, 0)

    @pl.when(active)
    def _():
        for peer in (chip_peer, y_peer, *q_peers):
            greet(peer)
        loop(0, SRC, lambda s: greet(source(s)))

    list_src[...] = jnp.full_like(list_src, -1)
    list_src[:, 0:SLOTS] = list_ref[...]
    stat[...] = jnp.zeros_like(stat)

    def spread(i, zcs):
        return (jnp.where(zc < 2, 2, 0) + i // 8) % zcs * 8 + (xh + 1 + i // 4) % 2 * 4 + (yh + 2 + i) % 4

    def send(which, h):
        pltpu.make_async_remote_copy(
            rows_in[which].at[:, pl.ds(pl.multiple_of(h * D, D), D)], held[which].at[mine], a_send.at[which], a_recv.at[which],
            device_id=target(h), device_id_type=MESH,
        ).start()

    def send_list(h):
        pltpu.make_async_remote_copy(
            list_src, lists.at[tile], a_send.at[3], a_recv.at[3], device_id=target(h), device_id_type=MESH
        ).start()

    @pl.when(active)
    def _():
        pl.semaphore_wait(barrier, HEADS + 5)

    @pl.when(jnp.logical_not(active))
    def _():
        pl.semaphore_wait(barrier, HEADS)

    @pl.when(xh == 0)
    def _():
        loop(0, HEADS, lambda i: send_list(spread(i, 3)))

    for which in range(3):
        loop(0, HEADS, lambda i: send(which, spread(i, 3)))

    def wait_for(ref, sem):
        pltpu.make_async_copy(ref, ref, sem).wait()

    @pl.when(active)
    def _():
        def block(which, place, half=None):
            low, size = (0, SRC) if half is None else (half * HALF, HALF)
            return held[which].at[pl.ds(place * SRC + low, size)]

        def swap(which, src, dst, i, dev, half=None):
            return pltpu.make_async_remote_copy(
                block(which, src, half), block(which, dst, half), b_send.at[which, i], b_recv.at[which, i],
                device_id=dev, device_id_type=MESH,
            )

        q_copies = [swap(0, 0, r, r - 1, q_peers[r - 1]) for r in range(1, 4)]
        y_copies = [[swap(which, 0, 2, half, y_peer, half) for half in range(2)] for which in (1, 2)]
        chip_copies = [swap(which, 0, 1, 2, chip_peer) for which in (1, 2)]
        on_copies = [[swap(which, 2, 3, 3 + half, chip_peer, half) for half in range(2)] for which in (1, 2)]

        def pass_on(i):
            for half in range(2):
                y_copies[i][half].wait_recv()
                on_copies[i][half].start()

        wait_for(block(0, 0), a_recv.at[0])
        for copy in q_copies:
            copy.start()

        wait_for(lists, a_recv.at[3])
        listed = lists[...]
        used[...] = jnp.broadcast_to(jnp.sum(jnp.where(listed >= 0, 1, 0), axis=2, keepdims=True), used.shape)
        listed = jnp.maximum(listed, 0)
        tile_yh = (listed >> 2) & 3
        tile_yl = ((listed >> 1) & 1) ^ jnp.where((tile_yh - yh) % 2 == 0, 1, 0)
        place = (tile_yl ^ yl) * 2 + ((listed & 1) ^ c)
        places[...] = place * SRC + tile_yh * 4 + (listed >> 4)
        to_scalars = pltpu.make_async_copy(places, places_s, list_sem)
        to_scalars.start()

        for which in (1, 2):
            wait_for(block(which, 0), a_recv.at[which])
            for copy in y_copies[which - 1]:
                copy.start()
            chip_copies[which - 1].start()
        pass_on(0)
        to_scalars.wait()
        for copy in q_copies + [chip_copies[0]] + on_copies[0]:
            copy.wait_recv()

        lane = lax.broadcasted_iota(jnp.int32, (D, D), 1)
        key_slot = lax.broadcasted_iota(jnp.int32, (1, 256), 1) % D // ROWS
        ones = jnp.ones((256, D), BF16)

        def gathered(which, t, g):
            blocks = [places_s[t, 0, s] for s in range(g * 8, g * 8 + 8)]
            return jnp.concatenate([held[which][b + half * HALF] for half in range(2) for b in blocks], axis=0)

        def weights_of(ts):
            scores = []
            for t in ts:
                limit = jnp.concatenate([used[t], used[t]], axis=1)
                query = jnp.concatenate([q_rows[r * SRC + half * HALF + t] for r in range(4) for half in range(2)], axis=0)
                scores.append([
                    lax.dot_general(query, gathered(1, t, g), (((1,), (1,)), ((), ())), preferred_element_type=F32)
                    + jnp.where(key_slot + g * 8 < limit, 0.0, LOW)
                    for g in range(4)
                ])
            found = []
            stats = stat[ts[0] // 8]
            for t, s in zip(ts, scores):
                top = jnp.maximum(jnp.maximum(s[0], s[1]), jnp.maximum(s[2], s[3]))
                top = jnp.max(top, axis=1, keepdims=True)
                stats = jnp.where(lane == t % 8, top, stats)
                found.append([jnp.exp2((s[g] - top) * SCALE).astype(BF16) for g in range(4)])
            stat[ts[0] // 8] = stats
            return found

        def numerators(ts, found):
            totals = []
            for t, w in zip(ts, found):
                total = jnp.zeros((D, 2 * D), F32)
                for g in range(4):
                    values = jnp.concatenate([gathered(2, t, g), ones], axis=1)
                    total = total + jnp.dot(w[g], values, preferred_element_type=F32)
                totals.append(total)
            stats = stat[ts[0] // 8]
            for t, total in zip(ts, totals):
                stats = jnp.where(lane == t % 8 + 64, total[:, D:], stats)
                numerator = total[:, :D].astype(BF16)
                for r in range(4):
                    for half in range(2):
                        low = r * PART + half * ROWS
                        part[r, half, t] = numerator[low : low + ROWS]
            stat[ts[0] // 8] = stats

        def part_copy(k, r):
            rows = pl.ds(k * PER_CHUNK, PER_CHUNK)
            return pltpu.make_async_remote_copy(
                part.at[r, :, rows], got.at[r - 1, :, rows], d_send.at[k, r - 1], d_recv.at[k, r - 1],
                device_id=q_peers[r - 1], device_id_type=MESH,
            )

        def pair(k):
            return [2 * k, 2 * k + 1]

        def send_parts(k):
            for r in range(1, 4):
                part_copy(k, r).start()

        def early_weights(k):
            for t, w in zip(pair(k), weights_of(pair(k))):
                for g in range(4):
                    kept[t, g] = w[g]

        def early_chunk(k):
            numerators(pair(k), [[kept[t, g] for g in range(4)] for t in pair(k)])
            send_parts(k)

        def chunk(k):
            numerators(pair(k), weights_of(pair(k)))
            send_parts(k)

        loop(0, EARLY // 2, early_weights)
        pass_on(1)
        loop(EARLY // 2, EARLY, early_weights)
        for copy in [chip_copies[1]] + on_copies[1]:
            copy.wait_recv()
        stat_copies = [
            [
                pltpu.make_async_remote_copy(
                    stat.at[g, pl.ds(r * PART, PART), :], got_stat.at[r - 1, g], s_send.at[g, r - 1], s_recv.at[g, r - 1],
                    device_id=q_peers[r - 1], device_id_type=MESH,
                )
                for r in range(1, 4)
            ]
            for g in range(2)
        ]
        loop(0, EARLY, early_chunk)
        for copy in stat_copies[0]:
            copy.start()
        loop(EARLY, CHUNKS, chunk)
        for copy in stat_copies[1]:
            copy.start()

        columns = out_ref.at[:, pl.ds(pl.multiple_of(head * D, D), D)]
        for k in range(CHUNKS):
            if k % 4 == 0:
                g = k // 4
                for copy in stat_copies[g]:
                    copy.wait_recv()
                stats = [stat[g, 0:PART, :]] + [got_stat[r, g] for r in range(3)]
                highest = jnp.maximum(jnp.maximum(stats[0], stats[1]), jnp.maximum(stats[2], stats[3]))
                factors = [jnp.exp2((s - highest) * SCALE) for s in stats]
                denominator = sum(f[:, 0:8] * s[:, 64:72] for f, s in zip(factors, stats))
                factors = [f[:, 0:8] / denominator for f in factors]
            for r in range(1, 4):
                part_copy(k, r).wait_recv()
            for t in pair(k):
                for half in range(2):
                    s = half * HALF + t
                    rows = slice(half * ROWS, (half + 1) * ROWS)
                    terms = [part[0, half, t]] + [got[r, half, t] for r in range(3)]
                    fin[s] = sum(f[rows, t % 8 : t % 8 + 1] * a.astype(F32) for f, a in zip(factors, terms)).astype(BF16)
                    pltpu.make_async_remote_copy(
                        fin.at[s], columns, e_sem.at[0], e_sem.at[1], device_id=source(s), device_id_type=MESH
                    ).start()

        for copy in q_copies + y_copies[0] + y_copies[1] + chip_copies + on_copies[0] + on_copies[1] + stat_copies[0] + stat_copies[1]:
            copy.wait_send()
        for k in range(CHUNKS):
            for r in range(1, 4):
                part_copy(k, r).wait_send()
        wait_for(fin, e_sem.at[0])

    for which in range(3):
        wait_for(rows_in[which], a_send.at[which])
    wait_for(out_ref, e_sem.at[1])

    @pl.when(xh == 0)
    def _():
        wait_for(list_room, a_send.at[3])


def per_device(query, key, value, tile_list):
    dma = pltpu.SemaphoreType.DMA
    return pl.pallas_call(
        kernel,
        out_shape=jax.ShapeDtypeStruct(query.shape, BF16),
        in_specs=[pl.BlockSpec(memory_space=pltpu.HBM)] * 3 + [pl.BlockSpec(memory_space=pltpu.VMEM)],
        out_specs=pl.BlockSpec(memory_space=pl.ANY),
        scratch_shapes=[
            pltpu.VMEM((1, D), jnp.int32),
            pltpu.VMEM((HEADS, 1, D), jnp.int32),
            pltpu.VMEM((TILES, 1, D), jnp.int32),
            pltpu.VMEM((TILES, 1, D), jnp.int32),
            pltpu.VMEM((TILES, 1, D), jnp.int32),
            pltpu.SMEM((TILES, 1, D), jnp.int32),
            pltpu.VMEM((4 * SRC, ROWS, D), BF16),
            pltpu.VMEM((4 * SRC, ROWS, D), BF16),
            pltpu.VMEM((4 * SRC, ROWS, D), BF16),
            pltpu.VMEM((2 * EARLY, 4, D, 256), BF16),
            pltpu.VMEM((4, 2, TILES, ROWS, D), BF16),
            pltpu.VMEM((3, 2, TILES, ROWS, D), BF16),
            pltpu.VMEM((2, D, D), F32),
            pltpu.VMEM((3, 2, PART, D), F32),
            pltpu.VMEM((SRC, ROWS, D), BF16),
            dma, dma((4,)), dma((4,)), dma((3, 5)), dma((3, 5)),
            dma((CHUNKS, 3)), dma((CHUNKS, 3)), dma((2, 3)), dma((2, 3)), dma((2,)),
        ],
        compiler_params=pltpu.CompilerParams(
            collective_id=0, has_side_effects=True, vmem_limit_bytes=56 * 1024 * 1024
        ),
        name="attention",
    )(query, key, value, tile_list)


def solution(mesh):
    rows = P(("blk", "uly"), None)
    return jax.shard_map(
        per_device,
        mesh=mesh,
        in_specs=(rows, rows, rows, P("blk", None)),
        out_specs=rows,
        check_vma=False,
    )
```

```python
import jax
import jax.numpy as jnp
from jax import lax
from jax.experimental import pallas as pl
from jax.experimental.pallas import tpu as pltpu
from jax.sharding import PartitionSpec as P

MESH = pl.DeviceIdType.MESH
D = 128
HEADS = 24
ROWS = 16
SRC = 32
TILES = 16
HALF = TILES
SLOTS = 32
PART = 32
CHUNKS = 8
PER_CHUNK = 2
SCALE = 1.4426950408889634 / 128**0.5
LOW = -1e30
F32, BF16 = jnp.float32, jnp.bfloat16


def kernel(
    q_hbm, k_hbm, v_hbm, list_ref, out_ref,
    list_room, lists, used, places, places_s, q_rows, k_rows, v_rows, part, got, stat, packed, got_stat, fin,
    list_sem, a_send, a_recv, b_send, b_recv, d_send, d_recv, s_send, s_recv, e_sem,
):
    blk, uly = lax.axis_index("blk"), lax.axis_index("uly")
    c, y, x = blk % 2, (blk // 2) % 8, uly // 2
    z = uly % 2 * 4 + blk // 16
    xh, xl, yh, yl, zc, zr = x // 2, x % 2, y // 2, y % 2, z // 2, z % 2
    active = zc < 3

    def device(x, y, z):
        return (((z % 4) * 8 + y) * 2 + c, x * 2 + z // 4)

    def turned(other):
        return jnp.where((other - yh) % 2 == 0, 1 - yl, yl)

    def crossed(other):
        return jnp.where(other == xh, xl, 1 - xl)

    def target(h):
        txh, tyh, tzc = h // 4 % 2, h % 4, h // 8
        zh = z // 4
        return device(2 * txh + crossed(txh), 2 * tyh + turned(tyh), 2 * tzc + jnp.where(tzc == 0, 1 - zh, zh))

    from_z = 4 * jnp.where(zc == 0, 1 - zr, zr)

    def source(s):
        sxh, syh = s // 16, s // 4 % 4
        return device(2 * sxh + crossed(sxh), 2 * syh + turned(syh), from_z + s % 4)

    head = zc * 8 + xh * 4 + yh
    tile = yh * 4 + z % 4
    mine = xh * HALF + tile

    rows_in = (q_hbm, k_hbm, v_hbm)
    held = (q_rows, k_rows, v_rows)

    def flip(value, by):
        return 1 - value if by else value

    chip_peer = (blk + 1 - 2 * c, uly)
    y_peer = device(x, 2 * yh + 1 - yl, z)
    q_peers = [device(2 * xh + flip(xl, r // 2), y, 2 * zc + flip(zr, r % 2)) for r in range(1, 4)]

    barrier = pltpu.get_barrier_semaphore()

    def greet(dev):
        pl.semaphore_signal(barrier, inc=1, device_id=dev, device_id_type=MESH)

    def loop(low, high, body):
        def step(i, carry):
            body(i)
            return carry

        lax.fori_loop(low, high, step, 0)

    @pl.when(active)
    def _():
        for peer in (chip_peer, y_peer, *q_peers):
            greet(peer)
        loop(0, SRC, lambda s: greet(source(s)))

    stat[...] = jnp.zeros_like(stat)

    def spread(i, zcs):
        return (jnp.where(zc < 2, 2, 0) + i // 8) % zcs * 8 + (xh + 1 + i // 4) % 2 * 4 + (yh + 2 + i) % 4

    def send(which, h):
        pltpu.make_async_remote_copy(
            rows_in[which].at[:, pl.ds(pl.multiple_of(h * D, D), D)], held[which].at[mine], a_send.at[which], a_recv.at[which],
            device_id=target(h), device_id_type=MESH,
        ).start()

    def send_list(h):
        pltpu.make_async_remote_copy(
            list_ref, lists.at[tile], a_send.at[3], a_recv.at[3], device_id=target(h), device_id_type=MESH
        ).start()

    @pl.when(active)
    def _():
        pl.semaphore_wait(barrier, HEADS + 5)

    @pl.when(jnp.logical_not(active))
    def _():
        pl.semaphore_wait(barrier, HEADS)

    @pl.when(xh == 0)
    def _():
        loop(0, HEADS, lambda i: send_list(spread(i, 3)))

    for which in range(3):
        loop(0, HEADS, lambda i: send(which, spread(i, 3)))

    def wait_for(ref, sem):
        pltpu.make_async_copy(ref, ref, sem).wait()

    @pl.when(active)
    def _():
        def block(which, place, half=None):
            low, size = (0, SRC) if half is None else (half * HALF, HALF)
            return held[which].at[pl.ds(place * SRC + low, size)]

        def swap(which, src, dst, i, dev, half=None):
            return pltpu.make_async_remote_copy(
                block(which, src, half), block(which, dst, half), b_send.at[which, i], b_recv.at[which, i],
                device_id=dev, device_id_type=MESH,
            )

        q_copies = [swap(0, 0, r, r - 1, q_peers[r - 1]) for r in range(1, 4)]
        y_copies = [[swap(which, 0, 2, half, y_peer, half) for half in range(2)] for which in (1, 2)]
        chip_copies = [swap(which, 0, 1, 2, chip_peer) for which in (1, 2)]
        on_copies = [[swap(which, 2, 3, 3 + half, chip_peer, half) for half in range(2)] for which in (1, 2)]

        def pass_on(i):
            for half in range(2):
                y_copies[i][half].wait_recv()
                on_copies[i][half].start()

        wait_for(block(0, 0), a_recv.at[0])
        for copy in q_copies:
            copy.start()

        wait_for(lists, a_recv.at[3])
        listed = lists[...]
        used[...] = jnp.broadcast_to(jnp.sum(jnp.where(listed >= 0, 1, 0), axis=2, keepdims=True), used.shape)
        listed = jnp.maximum(listed, 0)
        tile_yh = (listed >> 2) & 3
        tile_yl = ((listed >> 1) & 1) ^ jnp.where((tile_yh - yh) % 2 == 0, 1, 0)
        place = (tile_yl ^ yl) * 2 + ((listed & 1) ^ c)
        places[...] = place * SRC + tile_yh * 4 + (listed >> 4)
        to_scalars = pltpu.make_async_copy(places, places_s, list_sem)
        to_scalars.start()

        for which in (1, 2):
            wait_for(block(which, 0), a_recv.at[which])
            for copy in y_copies[which - 1]:
                copy.start()
            chip_copies[which - 1].start()
        pass_on(0)
        to_scalars.wait()
        for copy in q_copies + [chip_copies[0]] + on_copies[0]:
            copy.wait_recv()

        pass_on(1)
        for copy in [chip_copies[1]] + on_copies[1]:
            copy.wait_recv()

        lane = lax.broadcasted_iota(jnp.int32, (D, D), 1)
        key_slot = lax.broadcasted_iota(jnp.int32, (1, 256), 1) % D // ROWS
        ones = jnp.ones((256, D), BF16)

        def gathered(which, t, g):
            blocks = [places_s[t, 0, s] for s in range(g * 8, g * 8 + 8)]
            return jnp.concatenate([held[which][b + half * HALF] for half in range(2) for b in blocks], axis=0)

        def weights_of(ts):
            scores = []
            for t in ts:
                limit = jnp.concatenate([used[t], used[t]], axis=1)
                query = jnp.concatenate([q_rows[r * SRC + half * HALF + t] for r in range(4) for half in range(2)], axis=0)
                scores.append([
                    lax.dot_general(query, gathered(1, t, g), (((1,), (1,)), ((), ())), preferred_element_type=F32)
                    + jnp.where(key_slot + g * 8 < limit, 0.0, LOW)
                    for g in range(4)
                ])
            found = []
            stats = stat[ts[0] // 8]
            for t, s in zip(ts, scores):
                top = jnp.maximum(jnp.maximum(s[0], s[1]), jnp.maximum(s[2], s[3]))
                top = jnp.max(top, axis=1, keepdims=True)
                stats = jnp.where(lane == t % 8, top, stats)
                found.append([jnp.exp2((s[g] - top) * SCALE).astype(BF16) for g in range(4)])
            stat[ts[0] // 8] = stats
            return found

        def numerators(ts, found):
            totals = []
            for t, w in zip(ts, found):
                total = jnp.zeros((D, 2 * D), F32)
                for g in range(4):
                    values = jnp.concatenate([gathered(2, t, g), ones], axis=1)
                    total = total + jnp.dot(w[g], values, preferred_element_type=F32)
                totals.append(total)
            stats = stat[ts[0] // 8]
            for t, total in zip(ts, totals):
                stats = jnp.where(lane == t % 8 + 8, total[:, D:], stats)
                numerator = total[:, :D].astype(BF16)
                for r in range(4):
                    for half in range(2):
                        low = r * PART + half * ROWS
                        part[r, half, t] = numerator[low : low + ROWS]
            stat[ts[0] // 8] = stats

        def part_copy(k, r):
            rows = pl.ds(k * PER_CHUNK, PER_CHUNK)
            return pltpu.make_async_remote_copy(
                part.at[r, :, rows], got.at[r - 1, :, rows], d_send.at[k, r - 1], d_recv.at[k, r - 1],
                device_id=q_peers[r - 1], device_id_type=MESH,
            )

        def pair(k):
            return [2 * k, 2 * k + 1]

        def send_parts(k):
            for r in range(1, 4):
                part_copy(k, r).start()

        def chunk(k):
            numerators(pair(k), weights_of(pair(k)))
            send_parts(k)

        stat_copies = [
            [
                pltpu.make_async_remote_copy(
                    packed.at[r, g], got_stat.at[r - 1, g], s_send.at[g, r - 1], s_recv.at[g, r - 1],
                    device_id=q_peers[r - 1], device_id_type=MESH,
                )
                for r in range(1, 4)
            ]
            for g in range(2)
        ]

        def pack(g):
            for r in range(1, 4):
                parts = [stat[g, r * PART + 8 * i : r * PART + 8 * (i + 1), 0:32] for i in range(4)]
                packed[r, g] = jnp.concatenate(parts, axis=1)

        def unpacked(block):
            return jnp.concatenate([block[:, 32 * i : 32 * i + 16] for i in range(4)], axis=0)

        for g in range(2):
            loop(g * 4, g * 4 + 4, chunk)
            pack(g)
            for copy in stat_copies[g]:
                copy.start()

        columns = out_ref.at[:, pl.ds(pl.multiple_of(head * D, D), D)]
        for k in range(CHUNKS):
            if k % 4 == 0:
                g = k // 4
                for copy in stat_copies[g]:
                    copy.wait_recv()
                stats = [stat[g, 0:PART, 0:16]] + [unpacked(got_stat[r, g]) for r in range(3)]
                highest = jnp.maximum(jnp.maximum(stats[0], stats[1]), jnp.maximum(stats[2], stats[3]))
                factors = [jnp.exp2((s - highest) * SCALE) for s in stats]
                denominator = sum(f[:, 0:8] * s[:, 8:16] for f, s in zip(factors, stats))
                factors = [f[:, 0:8] / denominator for f in factors]
            for r in range(1, 4):
                part_copy(k, r).wait_recv()
            for t in pair(k):
                for half in range(2):
                    s = half * HALF + t
                    rows = slice(half * ROWS, (half + 1) * ROWS)
                    terms = [part[0, half, t]] + [got[r, half, t] for r in range(3)]
                    fin[s] = sum(f[rows, t % 8 : t % 8 + 1] * a.astype(F32) for f, a in zip(factors, terms)).astype(BF16)
                    pltpu.make_async_remote_copy(
                        fin.at[s], columns, e_sem.at[0], e_sem.at[1], device_id=source(s), device_id_type=MESH
                    ).start()

        for copy in q_copies + y_copies[0] + y_copies[1] + chip_copies + on_copies[0] + on_copies[1] + stat_copies[0] + stat_copies[1]:
            copy.wait_send()
        for k in range(CHUNKS):
            for r in range(1, 4):
                part_copy(k, r).wait_send()
        wait_for(fin, e_sem.at[0])

    for which in range(3):
        wait_for(rows_in[which], a_send.at[which])
    wait_for(out_ref, e_sem.at[1])

    @pl.when(xh == 0)
    def _():
        wait_for(list_room, a_send.at[3])


def per_device(query, key, value, tile_list):
    dma = pltpu.SemaphoreType.DMA
    return pl.pallas_call(
        kernel,
        out_shape=jax.ShapeDtypeStruct(query.shape, BF16),
        in_specs=[pl.BlockSpec(memory_space=pl.ANY)] * 4,
        out_specs=pl.BlockSpec(memory_space=pl.ANY),
        scratch_shapes=[
            pltpu.VMEM((HEADS, 1, SLOTS), jnp.int32),
            pltpu.VMEM((TILES, 1, SLOTS), jnp.int32),
            pltpu.VMEM((TILES, 1, D), jnp.int32),
            pltpu.VMEM((TILES, 1, SLOTS), jnp.int32),
            pltpu.SMEM((TILES, 1, SLOTS), jnp.int32),
            pltpu.VMEM((4 * SRC, ROWS, D), BF16),
            pltpu.VMEM((4 * SRC, ROWS, D), BF16),
            pltpu.VMEM((4 * SRC, ROWS, D), BF16),
            pltpu.VMEM((4, 2, TILES, ROWS, D), BF16),
            pltpu.VMEM((3, 2, TILES, ROWS, D), BF16),
            pltpu.VMEM((2, D, D), F32),
            pltpu.VMEM((4, 2, 8, D), F32),
            pltpu.VMEM((3, 2, 8, D), F32),
            pltpu.VMEM((SRC, ROWS, D), BF16),
            dma, dma((4,)), dma((4,)), dma((3, 5)), dma((3, 5)),
            dma((CHUNKS, 3)), dma((CHUNKS, 3)), dma((2, 3)), dma((2, 3)), dma((2,)),
        ],
        compiler_params=pltpu.CompilerParams(
            collective_id=0, has_side_effects=True, vmem_limit_bytes=56393728
        ),
        name="attention",
    )(query, key, value, tile_list)


def solution(mesh):
    rows = P(("blk", "uly"), None)
    return jax.shard_map(
        per_device,
        mesh=mesh,
        in_specs=(rows, rows, rows, P("blk", None)),
        out_specs=rows,
        check_vma=False,
    )
```

```python
import jax
import jax.numpy as jnp
from jax import lax
from jax.experimental import pallas as pl
from jax.experimental.pallas import tpu as pltpu
from jax.sharding import PartitionSpec as P

MESH = pl.DeviceIdType.MESH
D = 128
HEADS = 24
ROWS = 16
SRC = 32
TILES = 16
HALF = TILES
SLOTS = 32
PART = 32
CHUNKS = 8
PER_CHUNK = 2
SCALE = 1.4426950408889634 / 128**0.5
LOW = -1e30
F32, BF16 = jnp.float32, jnp.bfloat16


def kernel(
    q_hbm, k_hbm, v_hbm, list_ref, out_ref,
    list_room, lists, used, places, places_s, q_rows, k_rows, v_rows, part, got, stat, packed, got_stat, fin,
    list_sem, a_send, a_recv, b_send, b_recv, d_send, d_recv, s_send, s_recv, e_sem,
):
    blk, uly = lax.axis_index("blk"), lax.axis_index("uly")
    c, y, x = blk % 2, (blk // 2) % 8, uly // 2
    z = uly % 2 * 4 + blk // 16
    xh, xl, yh, yl, zc, zr = x // 2, x % 2, y // 2, y % 2, z // 2, z % 2
    active = zc < 3

    def device(x, y, z):
        return (((z % 4) * 8 + y) * 2 + c, x * 2 + z // 4)

    def turned(other):
        return jnp.where((other - yh) % 2 == 0, 1 - yl, yl)

    def crossed(other):
        return jnp.where(other == xh, xl, 1 - xl)

    def target(h):
        txh, tyh, tzc = h // 4 % 2, h % 4, h // 8
        zh = z // 4
        return device(2 * txh + crossed(txh), 2 * tyh + turned(tyh), 2 * tzc + jnp.where(tzc == 0, 1 - zh, zh))

    from_z = 4 * jnp.where(zc == 0, 1 - zr, zr)

    def source(s):
        sxh, syh = s // 16, s % 4
        return device(2 * sxh + crossed(sxh), 2 * syh + turned(syh), from_z + s // 4 % 4)

    head = zc * 8 + xh * 4 + yh
    tile = z % 4 * 4 + yh
    mine = xh * HALF + tile

    rows_in = (q_hbm, k_hbm, v_hbm)
    held = (q_rows, k_rows, v_rows)

    def flip(value, by):
        return 1 - value if by else value

    chip_peer = (blk + 1 - 2 * c, uly)
    y_peer = device(x, 2 * yh + 1 - yl, z)
    q_peers = [device(2 * xh + flip(xl, r // 2), y, 2 * zc + flip(zr, r % 2)) for r in range(1, 4)]

    barrier = pltpu.get_barrier_semaphore()

    def greet(dev):
        pl.semaphore_signal(barrier, inc=1, device_id=dev, device_id_type=MESH)

    def loop(low, high, body):
        def step(i, carry):
            body(i)
            return carry

        lax.fori_loop(low, high, step, 0)

    @pl.when(active)
    def _():
        for peer in (chip_peer, y_peer, *q_peers):
            greet(peer)
        loop(0, SRC, lambda s: greet(source(s)))

    stat[...] = jnp.zeros_like(stat)

    def spread(i, zcs):
        return (jnp.where(zc < 2, 2, 0) + i // 8) % zcs * 8 + (xh + 1 + i // 4) % 2 * 4 + (yh + 2 + i) % 4

    def send(which, h):
        pltpu.make_async_remote_copy(
            rows_in[which].at[:, pl.ds(pl.multiple_of(h * D, D), D)], held[which].at[mine], a_send.at[which], a_recv.at[which],
            device_id=target(h), device_id_type=MESH,
        ).start()

    def send_list(h):
        pltpu.make_async_remote_copy(
            list_ref, lists.at[tile], a_send.at[3], a_recv.at[3], device_id=target(h), device_id_type=MESH
        ).start()

    @pl.when(active)
    def _():
        pl.semaphore_wait(barrier, HEADS + 5)

    @pl.when(jnp.logical_not(active))
    def _():
        pl.semaphore_wait(barrier, HEADS)

    @pl.when(xh == 0)
    def _():
        loop(0, HEADS, lambda i: send_list(spread(i, 3)))

    for which in range(3):
        loop(0, HEADS, lambda i: send(which, spread(i, 3)))

    def wait_for(ref, sem):
        pltpu.make_async_copy(ref, ref, sem).wait()

    @pl.when(active)
    def _():
        def block(which, place, half=None):
            low, size = (0, SRC) if half is None else (half * HALF, HALF)
            return held[which].at[pl.ds(place * SRC + low, size)]

        def swap(which, src, dst, i, dev, half=None):
            return pltpu.make_async_remote_copy(
                block(which, src, half), block(which, dst, half), b_send.at[which, i], b_recv.at[which, i],
                device_id=dev, device_id_type=MESH,
            )

        q_copies = [swap(0, 0, r, r - 1, q_peers[r - 1]) for r in range(1, 4)]
        y_copies = [[swap(which, 0, 2, half, y_peer, half) for half in range(2)] for which in (1, 2)]
        chip_copies = [swap(which, 0, 1, 2, chip_peer) for which in (1, 2)]
        on_copies = [[swap(which, 2, 3, 3 + half, chip_peer, half) for half in range(2)] for which in (1, 2)]

        def pass_on(i):
            for half in range(2):
                y_copies[i][half].wait_recv()
                on_copies[i][half].start()

        wait_for(block(0, 0), a_recv.at[0])
        for copy in q_copies:
            copy.start()

        wait_for(lists, a_recv.at[3])
        listed = lists[...]
        used[...] = jnp.broadcast_to(jnp.sum(jnp.where(listed >= 0, 1, 0), axis=2, keepdims=True), used.shape)
        listed = jnp.maximum(listed, 0)
        tile_yh = (listed >> 2) & 3
        tile_yl = ((listed >> 1) & 1) ^ jnp.where((tile_yh - yh) % 2 == 0, 1, 0)
        place = (tile_yl ^ yl) * 2 + ((listed & 1) ^ c)
        places[...] = place * SRC + (listed >> 4) * 4 + tile_yh
        to_scalars = pltpu.make_async_copy(places, places_s, list_sem)
        to_scalars.start()

        for which in (1, 2):
            wait_for(block(which, 0), a_recv.at[which])
            for copy in y_copies[which - 1]:
                copy.start()
            chip_copies[which - 1].start()
        pass_on(0)
        to_scalars.wait()
        for copy in q_copies + [chip_copies[0]] + on_copies[0]:
            copy.wait_recv()

        pass_on(1)
        for copy in [chip_copies[1]] + on_copies[1]:
            copy.wait_recv()

        lane = lax.broadcasted_iota(jnp.int32, (D, D), 1)
        key_slot = lax.broadcasted_iota(jnp.int32, (1, 256), 1) % D // ROWS
        ones = jnp.ones((256, D), BF16)

        def gathered(which, t, g):
            blocks = [places_s[t, 0, s] for s in range(g * 8, g * 8 + 8)]
            return jnp.concatenate([held[which][b + half * HALF] for half in range(2) for b in blocks], axis=0)

        def weights_of(ts):
            scores = []
            for t in ts:
                limit = jnp.concatenate([used[t], used[t]], axis=1)
                query = jnp.concatenate([q_rows[r * SRC + half * HALF + t] for r in range(4) for half in range(2)], axis=0)
                scores.append([
                    lax.dot_general(query, gathered(1, t, g), (((1,), (1,)), ((), ())), preferred_element_type=F32)
                    + jnp.where(key_slot + g * 8 < limit, 0.0, LOW)
                    for g in range(4)
                ])
            found = []
            stats = stat[ts[0] // 8]
            for t, s in zip(ts, scores):
                top = jnp.maximum(jnp.maximum(s[0], s[1]), jnp.maximum(s[2], s[3]))
                top = jnp.max(top, axis=1, keepdims=True)
                stats = jnp.where(lane == t % 8, top, stats)
                found.append([jnp.exp2((s[g] - top) * SCALE).astype(BF16) for g in range(4)])
            stat[ts[0] // 8] = stats
            return found

        def numerators(ts, found):
            totals = []
            for t, w in zip(ts, found):
                total = jnp.zeros((D, 2 * D), F32)
                for g in range(4):
                    values = jnp.concatenate([gathered(2, t, g), ones], axis=1)
                    total = total + jnp.dot(w[g], values, preferred_element_type=F32)
                totals.append(total)
            stats = stat[ts[0] // 8]
            for t, total in zip(ts, totals):
                stats = jnp.where(lane == t % 8 + 8, total[:, D:], stats)
                numerator = total[:, :D].astype(BF16)
                for r in range(4):
                    for half in range(2):
                        low = r * PART + half * ROWS
                        part[r, half, t] = numerator[low : low + ROWS]
            stat[ts[0] // 8] = stats

        def part_copy(k, r):
            rows = pl.ds(k * PER_CHUNK, PER_CHUNK)
            return pltpu.make_async_remote_copy(
                part.at[r, :, rows], got.at[r - 1, :, rows], d_send.at[k, r - 1], d_recv.at[k, r - 1],
                device_id=q_peers[r - 1], device_id_type=MESH,
            )

        def pair(k):
            return [2 * k, 2 * k + 1]

        def send_parts(k):
            for r in range(1, 4):
                part_copy(k, r).start()

        def chunk(k):
            numerators(pair(k), weights_of(pair(k)))
            send_parts(k)

        stat_copies = [
            [
                pltpu.make_async_remote_copy(
                    packed.at[r, g], got_stat.at[r - 1, g], s_send.at[g, r - 1], s_recv.at[g, r - 1],
                    device_id=q_peers[r - 1], device_id_type=MESH,
                )
                for r in range(1, 4)
            ]
            for g in range(2)
        ]

        def pack(g):
            for r in range(1, 4):
                parts = [stat[g, r * PART + 8 * i : r * PART + 8 * (i + 1), 0:32] for i in range(4)]
                packed[r, g] = jnp.concatenate(parts, axis=1)

        def unpacked(block):
            return jnp.concatenate([block[:, 32 * i : 32 * i + 16] for i in range(4)], axis=0)

        for g in range(2):
            loop(g * 4, g * 4 + 4, chunk)
            pack(g)
            for copy in stat_copies[g]:
                copy.start()

        columns = out_ref.at[:, pl.ds(pl.multiple_of(head * D, D), D)]
        for k in range(CHUNKS):
            if k % 4 == 0:
                g = k // 4
                for copy in stat_copies[g]:
                    copy.wait_recv()
                stats = [stat[g, 0:PART, 0:16]] + [unpacked(got_stat[r, g]) for r in range(3)]
                highest = jnp.maximum(jnp.maximum(stats[0], stats[1]), jnp.maximum(stats[2], stats[3]))
                factors = [jnp.exp2((s - highest) * SCALE) for s in stats]
                denominator = sum(f[:, 0:8] * s[:, 8:16] for f, s in zip(factors, stats))
                factors = [f[:, 0:8] / denominator for f in factors]
            for r in range(1, 4):
                part_copy(k, r).wait_recv()
            for t in pair(k):
                for half in range(2):
                    s = half * HALF + t
                    rows = slice(half * ROWS, (half + 1) * ROWS)
                    terms = [part[0, half, t]] + [got[r, half, t] for r in range(3)]
                    fin[s] = sum(f[rows, t % 8 : t % 8 + 1] * a.astype(F32) for f, a in zip(factors, terms)).astype(BF16)
                    pltpu.make_async_remote_copy(
                        fin.at[s], columns, e_sem.at[0], e_sem.at[1], device_id=source(s), device_id_type=MESH
                    ).start()

        for copy in q_copies + y_copies[0] + y_copies[1] + chip_copies + on_copies[0] + on_copies[1] + stat_copies[0] + stat_copies[1]:
            copy.wait_send()
        for k in range(CHUNKS):
            for r in range(1, 4):
                part_copy(k, r).wait_send()
        wait_for(fin, e_sem.at[0])

    for which in range(3):
        wait_for(rows_in[which], a_send.at[which])
    wait_for(out_ref, e_sem.at[1])

    @pl.when(xh == 0)
    def _():
        wait_for(list_room, a_send.at[3])


def per_device(query, key, value, tile_list):
    dma = pltpu.SemaphoreType.DMA
    return pl.pallas_call(
        kernel,
        out_shape=jax.ShapeDtypeStruct(query.shape, BF16),
        in_specs=[pl.BlockSpec(memory_space=pl.ANY)] * 4,
        out_specs=pl.BlockSpec(memory_space=pl.ANY),
        scratch_shapes=[
            pltpu.VMEM((HEADS, 1, SLOTS), jnp.int32),
            pltpu.VMEM((TILES, 1, SLOTS), jnp.int32),
            pltpu.VMEM((TILES, 1, D), jnp.int32),
            pltpu.VMEM((TILES, 1, SLOTS), jnp.int32),
            pltpu.SMEM((TILES, 1, SLOTS), jnp.int32),
            pltpu.VMEM((4 * SRC, ROWS, D), BF16),
            pltpu.VMEM((4 * SRC, ROWS, D), BF16),
            pltpu.VMEM((4 * SRC, ROWS, D), BF16),
            pltpu.VMEM((4, 2, TILES, ROWS, D), BF16),
            pltpu.VMEM((3, 2, TILES, ROWS, D), BF16),
            pltpu.VMEM((2, D, D), F32),
            pltpu.VMEM((4, 2, 8, D), F32),
            pltpu.VMEM((3, 2, 8, D), F32),
            pltpu.VMEM((SRC, ROWS, D), BF16),
            dma, dma((4,)), dma((4,)), dma((3, 5)), dma((3, 5)),
            dma((CHUNKS, 3)), dma((CHUNKS, 3)), dma((2, 3)), dma((2, 3)), dma((2,)),
        ],
        compiler_params=pltpu.CompilerParams(
            collective_id=0, has_side_effects=True, vmem_limit_bytes=56393728
        ),
        name="attention",
    )(query, key, value, tile_list)


def solution(mesh):
    rows = P(("blk", "uly"), None)
    return jax.shard_map(
        per_device,
        mesh=mesh,
        in_specs=(rows, rows, rows, P("blk", None)),
        out_specs=rows,
        check_vma=False,
    )
```

```python
import jax
import jax.numpy as jnp
from jax import lax
from jax.experimental import pallas as pl
from jax.experimental.pallas import tpu as pltpu
from jax.sharding import PartitionSpec as P

MESH = pl.DeviceIdType.MESH
D = 128
HEADS = 24
ROWS = 16
SRC = 32
TILES = 16
HALF = TILES
SLOTS = 32
PART = 32
CHUNKS = 8
PER_CHUNK = 2
SCALE = 1.4426950408889634 / 128**0.5
LOW = -1e30
F32, BF16 = jnp.float32, jnp.bfloat16


def kernel(
    q_hbm, k_hbm, v_hbm, list_ref, out_ref,
    list_room, lists, used, places, places_s, q_rows, k_rows, v_rows, part, got, stat, packed, got_stat, fin,
    list_sem, a_send, a_recv, b_send, b_recv, d_send, d_recv, s_send, s_recv, e_sem,
):
    blk, uly = lax.axis_index("blk"), lax.axis_index("uly")
    c, y, x = blk % 2, (blk // 2) % 8, uly // 2
    z = uly % 2 * 4 + blk // 16
    xh, xl, yh, yl, zc, zr = x // 2, x % 2, y // 2, y % 2, z // 2, z % 2
    active = zc < 3

    def device(x, y, z):
        return (((z % 4) * 8 + y) * 2 + c, x * 2 + z // 4)

    def turned(other):
        return jnp.where((other - yh) % 2 == 0, 1 - yl, yl)

    def crossed(other):
        return jnp.where(other == xh, xl, 1 - xl)

    def target(h):
        txh, tyh, tzc = h // 4 % 2, h % 4, h // 8
        zh = z // 4
        return device(2 * txh + crossed(txh), 2 * tyh + turned(tyh), 2 * tzc + jnp.where(tzc == 0, 1 - zh, zh))

    from_z = 4 * jnp.where(zc == 0, 1 - zr, zr)

    def source(s):
        sxh, syh = s // 16, s % 4
        return device(2 * sxh + crossed(sxh), 2 * syh + turned(syh), from_z + s // 4 % 4)

    head = zc * 8 + xh * 4 + yh
    tile = z % 4 * 4 + yh
    mine = xh * HALF + tile

    rows_in = (q_hbm, k_hbm, v_hbm)
    held = (q_rows, k_rows, v_rows)

    def flip(value, by):
        return 1 - value if by else value

    chip_peer = (blk + 1 - 2 * c, uly)
    y_peer = device(x, 2 * yh + 1 - yl, z)
    q_peers = [device(2 * xh + flip(xl, r // 2), y, 2 * zc + flip(zr, r % 2)) for r in range(1, 4)]

    barrier = pltpu.get_barrier_semaphore()

    def greet(dev):
        pl.semaphore_signal(barrier, inc=1, device_id=dev, device_id_type=MESH)

    def loop(low, high, body):
        def step(i, carry):
            body(i)
            return carry

        lax.fori_loop(low, high, step, 0)

    @pl.when(active)
    def _():
        for peer in (chip_peer, y_peer, *q_peers):
            greet(peer)
        loop(0, SRC, lambda s: greet(source(s)))

    stat[...] = jnp.zeros_like(stat)

    def spread(i, zcs):
        return (jnp.where(zc < 2, 2, 0) + i // 8) % zcs * 8 + (xh + 1 + i // 4) % 2 * 4 + (yh + 2 + i) % 4

    def send(which, h):
        pltpu.make_async_remote_copy(
            rows_in[which].at[:, pl.ds(pl.multiple_of(h * D, D), D)], held[which].at[mine], a_send.at[which], a_recv.at[which],
            device_id=target(h), device_id_type=MESH,
        ).start()

    def send_list(h):
        pltpu.make_async_remote_copy(
            list_ref, lists.at[tile], a_send.at[3], a_recv.at[3], device_id=target(h), device_id_type=MESH
        ).start()

    @pl.when(active)
    def _():
        pl.semaphore_wait(barrier, HEADS + 5)

    @pl.when(jnp.logical_not(active))
    def _():
        pl.semaphore_wait(barrier, HEADS)

    for which in range(3):
        loop(0, HEADS, lambda i: send(which, spread(i, 3)))

    @pl.when(xh == 0)
    def _():
        loop(0, HEADS, lambda i: send_list(spread(i, 3)))

    def wait_for(ref, sem):
        pltpu.make_async_copy(ref, ref, sem).wait()

    @pl.when(active)
    def _():
        def block(which, place, half=None):
            low, size = (0, SRC) if half is None else (half * HALF, HALF)
            return held[which].at[pl.ds(place * SRC + low, size)]

        def swap(which, src, dst, i, dev, half=None):
            return pltpu.make_async_remote_copy(
                block(which, src, half), block(which, dst, half), b_send.at[which, i], b_recv.at[which, i],
                device_id=dev, device_id_type=MESH,
            )

        q_copies = [swap(0, 0, r, r - 1, q_peers[r - 1]) for r in range(1, 4)]
        y_copies = [[swap(which, 0, 2, half, y_peer, half) for half in range(2)] for which in (1, 2)]
        chip_copies = [swap(which, 0, 1, 2, chip_peer) for which in (1, 2)]
        on_copies = [[swap(which, 2, 3, 3 + half, chip_peer, half) for half in range(2)] for which in (1, 2)]

        def pass_on(i):
            for half in range(2):
                y_copies[i][half].wait_recv()
                on_copies[i][half].start()

        wait_for(block(0, 0), a_recv.at[0])
        for copy in q_copies:
            copy.start()

        for which in (1, 2):
            wait_for(block(which, 0), a_recv.at[which])
            for copy in y_copies[which - 1]:
                copy.start()
            chip_copies[which - 1].start()

        wait_for(lists, a_recv.at[3])
        listed = lists[...]
        used[...] = jnp.broadcast_to(jnp.sum(jnp.where(listed >= 0, 1, 0), axis=2, keepdims=True), used.shape)
        listed = jnp.maximum(listed, 0)
        tile_yh = (listed >> 2) & 3
        tile_yl = ((listed >> 1) & 1) ^ jnp.where((tile_yh - yh) % 2 == 0, 1, 0)
        place = (tile_yl ^ yl) * 2 + ((listed & 1) ^ c)
        places[...] = place * SRC + (listed >> 4) * 4 + tile_yh
        to_scalars = pltpu.make_async_copy(places, places_s, list_sem)
        to_scalars.start()

        pass_on(0)
        to_scalars.wait()
        for copy in q_copies + [chip_copies[0]] + on_copies[0]:
            copy.wait_recv()

        pass_on(1)
        for copy in [chip_copies[1]] + on_copies[1]:
            copy.wait_recv()

        lane = lax.broadcasted_iota(jnp.int32, (D, D), 1)
        key_slot = lax.broadcasted_iota(jnp.int32, (1, 256), 1) % D // ROWS
        ones = jnp.ones((256, D), BF16)

        def gathered(which, t, g):
            blocks = [places_s[t, 0, s] for s in range(g * 8, g * 8 + 8)]
            return jnp.concatenate([held[which][b + half * HALF] for half in range(2) for b in blocks], axis=0)

        def weights_of(ts):
            scores = []
            for t in ts:
                limit = jnp.concatenate([used[t], used[t]], axis=1)
                query = jnp.concatenate([q_rows[r * SRC + half * HALF + t] for r in range(4) for half in range(2)], axis=0)
                scores.append([
                    lax.dot_general(query, gathered(1, t, g), (((1,), (1,)), ((), ())), preferred_element_type=F32)
                    + jnp.where(key_slot + g * 8 < limit, 0.0, LOW)
                    for g in range(4)
                ])
            found = []
            stats = stat[ts[0] // 8]
            for t, s in zip(ts, scores):
                top = jnp.maximum(jnp.maximum(s[0], s[1]), jnp.maximum(s[2], s[3]))
                top = jnp.max(top, axis=1, keepdims=True)
                stats = jnp.where(lane == t % 8, top, stats)
                found.append([jnp.exp2((s[g] - top) * SCALE).astype(BF16) for g in range(4)])
            stat[ts[0] // 8] = stats
            return found

        def numerators(ts, found):
            totals = []
            for t, w in zip(ts, found):
                total = jnp.zeros((D, 2 * D), F32)
                for g in range(4):
                    values = jnp.concatenate([gathered(2, t, g), ones], axis=1)
                    total = total + jnp.dot(w[g], values, preferred_element_type=F32)
                totals.append(total)
            stats = stat[ts[0] // 8]
            for t, total in zip(ts, totals):
                stats = jnp.where(lane == t % 8 + 8, total[:, D:], stats)
                numerator = total[:, :D].astype(BF16)
                for r in range(4):
                    for half in range(2):
                        low = r * PART + half * ROWS
                        part[r, half, t] = numerator[low : low + ROWS]
            stat[ts[0] // 8] = stats

        def part_copy(k, r):
            rows = pl.ds(k * PER_CHUNK, PER_CHUNK)
            return pltpu.make_async_remote_copy(
                part.at[r, :, rows], got.at[r - 1, :, rows], d_send.at[k, r - 1], d_recv.at[k, r - 1],
                device_id=q_peers[r - 1], device_id_type=MESH,
            )

        def pair(k):
            return [2 * k, 2 * k + 1]

        def send_parts(k):
            for r in range(1, 4):
                part_copy(k, r).start()

        def chunk(k):
            numerators(pair(k), weights_of(pair(k)))
            send_parts(k)

        stat_copies = [
            [
                pltpu.make_async_remote_copy(
                    packed.at[r, g], got_stat.at[r - 1, g], s_send.at[g, r - 1], s_recv.at[g, r - 1],
                    device_id=q_peers[r - 1], device_id_type=MESH,
                )
                for r in range(1, 4)
            ]
            for g in range(2)
        ]

        def pack(g):
            for r in range(1, 4):
                parts = [stat[g, r * PART + 8 * i : r * PART + 8 * (i + 1), 0:32] for i in range(4)]
                packed[r, g] = jnp.concatenate(parts, axis=1)

        def unpacked(block):
            return jnp.concatenate([block[:, 32 * i : 32 * i + 16] for i in range(4)], axis=0)

        for g in range(2):
            loop(g * 4, g * 4 + 4, chunk)
            pack(g)
            for copy in stat_copies[g]:
                copy.start()

        columns = out_ref.at[:, pl.ds(pl.multiple_of(head * D, D), D)]
        for k in range(CHUNKS):
            if k % 4 == 0:
                g = k // 4
                for copy in stat_copies[g]:
                    copy.wait_recv()
                stats = [stat[g, 0:PART, 0:16]] + [unpacked(got_stat[r, g]) for r in range(3)]
                highest = jnp.maximum(jnp.maximum(stats[0], stats[1]), jnp.maximum(stats[2], stats[3]))
                factors = [jnp.exp2((s - highest) * SCALE) for s in stats]
                denominator = sum(f[:, 0:8] * s[:, 8:16] for f, s in zip(factors, stats))
                factors = [f[:, 0:8] / denominator for f in factors]
            for r in range(1, 4):
                part_copy(k, r).wait_recv()
            for t in pair(k):
                for half in range(2):
                    s = half * HALF + t
                    rows = slice(half * ROWS, (half + 1) * ROWS)
                    terms = [part[0, half, t]] + [got[r, half, t] for r in range(3)]
                    fin[s] = sum(f[rows, t % 8 : t % 8 + 1] * a.astype(F32) for f, a in zip(factors, terms)).astype(BF16)
                    pltpu.make_async_remote_copy(
                        fin.at[s], columns, e_sem.at[0], e_sem.at[1], device_id=source(s), device_id_type=MESH
                    ).start()

        for copy in q_copies + y_copies[0] + y_copies[1] + chip_copies + on_copies[0] + on_copies[1] + stat_copies[0] + stat_copies[1]:
            copy.wait_send()
        for k in range(CHUNKS):
            for r in range(1, 4):
                part_copy(k, r).wait_send()
        wait_for(fin, e_sem.at[0])

    for which in range(3):
        wait_for(rows_in[which], a_send.at[which])
    wait_for(out_ref, e_sem.at[1])

    @pl.when(xh == 0)
    def _():
        wait_for(list_room, a_send.at[3])


def per_device(query, key, value, tile_list):
    dma = pltpu.SemaphoreType.DMA
    return pl.pallas_call(
        kernel,
        out_shape=jax.ShapeDtypeStruct(query.shape, BF16),
        in_specs=[pl.BlockSpec(memory_space=pl.ANY)] * 4,
        out_specs=pl.BlockSpec(memory_space=pl.ANY),
        scratch_shapes=[
            pltpu.VMEM((HEADS, 1, SLOTS), jnp.int32),
            pltpu.VMEM((TILES, 1, SLOTS), jnp.int32),
            pltpu.VMEM((TILES, 1, D), jnp.int32),
            pltpu.VMEM((TILES, 1, SLOTS), jnp.int32),
            pltpu.SMEM((TILES, 1, SLOTS), jnp.int32),
            pltpu.VMEM((4 * SRC, ROWS, D), BF16),
            pltpu.VMEM((4 * SRC, ROWS, D), BF16),
            pltpu.VMEM((4 * SRC, ROWS, D), BF16),
            pltpu.VMEM((4, 2, TILES, ROWS, D), BF16),
            pltpu.VMEM((3, 2, TILES, ROWS, D), BF16),
            pltpu.VMEM((2, D, D), F32),
            pltpu.VMEM((4, 2, 8, D), F32),
            pltpu.VMEM((3, 2, 8, D), F32),
            pltpu.VMEM((SRC, ROWS, D), BF16),
            dma, dma((4,)), dma((4,)), dma((3, 5)), dma((3, 5)),
            dma((CHUNKS, 3)), dma((CHUNKS, 3)), dma((2, 3)), dma((2, 3)), dma((2,)),
        ],
        compiler_params=pltpu.CompilerParams(
            collective_id=0, has_side_effects=True, vmem_limit_bytes=56393728
        ),
        name="attention",
    )(query, key, value, tile_list)


def solution(mesh):
    rows = P(("blk", "uly"), None)
    return jax.shard_map(
        per_device,
        mesh=mesh,
        in_specs=(rows, rows, rows, P("blk", None)),
        out_specs=rows,
        check_vma=False,
    )
```

```python
import jax
import jax.numpy as jnp
from jax import lax
from jax.experimental import pallas as pl
from jax.experimental.pallas import tpu as pltpu
from jax.sharding import PartitionSpec as P

MESH = pl.DeviceIdType.MESH
D = 128
HEADS = 24
ROWS = 16
SRC = 32
TILES = 16
HALF = TILES
SLOTS = 32
PART = 32
CHUNKS = 8
PER_CHUNK = 2
SCALE = 1.4426950408889634 / 128**0.5
LOW = -1e30
F32, BF16 = jnp.float32, jnp.bfloat16


def kernel(
    q_hbm, k_hbm, v_hbm, list_ref, out_ref,
    list_room, lists, used, places, places_s, q_rows, k_rows, v_rows, part, got, stat, packed, got_stat, fin,
    list_sem, a_send, a_recv, b_send, b_recv, d_send, d_recv, s_send, s_recv, e_sem,
):
    blk, uly = lax.axis_index("blk"), lax.axis_index("uly")
    c, y, x = blk % 2, (blk // 2) % 8, uly // 2
    z = uly % 2 * 4 + blk // 16
    xh, xl, yh, yl, zc, zr = x // 2, x % 2, y // 2, y % 2, z // 2, z % 2
    active = zc < 3

    def device(x, y, z):
        return (((z % 4) * 8 + y) * 2 + c, x * 2 + z // 4)

    def turned(other):
        return jnp.where((other - yh) % 2 == 0, 1 - yl, yl)

    def crossed(other):
        return jnp.where(other == xh, xl, 1 - xl)

    def target(h):
        txh, tyh, tzc = h // 4 % 2, h % 4, h // 8
        zh = z // 4
        return device(2 * txh + crossed(txh), 2 * tyh + turned(tyh), 2 * tzc + jnp.where(tzc == 0, 1 - zh, zh))

    from_z = 4 * jnp.where(zc == 0, 1 - zr, zr)

    def source(s):
        sxh, syh = s // 16, s % 4
        return device(2 * sxh + crossed(sxh), 2 * syh + turned(syh), from_z + s // 4 % 4)

    head = zc * 8 + xh * 4 + yh
    tile = z % 4 * 4 + yh
    mine = xh * HALF + tile

    rows_in = (q_hbm, k_hbm, v_hbm)
    held = (q_rows, k_rows, v_rows)

    def flip(value, by):
        return 1 - value if by else value

    chip_peer = (blk + 1 - 2 * c, uly)
    y_peer = device(x, 2 * yh + 1 - yl, z)
    q_peers = [device(2 * xh + flip(xl, r // 2), y, 2 * zc + flip(zr, r % 2)) for r in range(1, 4)]

    barrier = pltpu.get_barrier_semaphore()

    def greet(dev):
        pl.semaphore_signal(barrier, inc=1, device_id=dev, device_id_type=MESH)

    def loop(low, high, body):
        def step(i, carry):
            body(i)
            return carry

        lax.fori_loop(low, high, step, 0)

    @pl.when(active)
    def _():
        for peer in (chip_peer, y_peer, *q_peers):
            greet(peer)
        loop(0, SRC, lambda s: greet(source(s)))

    stat[...] = jnp.zeros_like(stat)

    def spread(i, zcs):
        return (jnp.where(zc < 2, 2, 0) + i // 4) % zcs * 8 + (xh + 1 + i // 12) % 2 * 4 + (yh + 2 + i) % 4

    def send(which, h):
        pltpu.make_async_remote_copy(
            rows_in[which].at[:, pl.ds(pl.multiple_of(h * D, D), D)], held[which].at[mine], a_send.at[which], a_recv.at[which],
            device_id=target(h), device_id_type=MESH,
        ).start()

    def send_list(h):
        pltpu.make_async_remote_copy(
            list_ref, lists.at[tile], a_send.at[3], a_recv.at[3], device_id=target(h), device_id_type=MESH
        ).start()

    @pl.when(active)
    def _():
        pl.semaphore_wait(barrier, HEADS + 5)

    @pl.when(jnp.logical_not(active))
    def _():
        pl.semaphore_wait(barrier, HEADS)

    for which in range(3):
        loop(0, HEADS, lambda i: send(which, spread(i, 3)))

    @pl.when(xh == 0)
    def _():
        loop(0, HEADS, lambda i: send_list(spread(i, 3)))

    def wait_for(ref, sem):
        pltpu.make_async_copy(ref, ref, sem).wait()

    @pl.when(active)
    def _():
        def block(which, place, half=None):
            low, size = (0, SRC) if half is None else (half * HALF, HALF)
            return held[which].at[pl.ds(place * SRC + low, size)]

        def swap(which, src, dst, i, dev, half=None):
            return pltpu.make_async_remote_copy(
                block(which, src, half), block(which, dst, half), b_send.at[which, i], b_recv.at[which, i],
                device_id=dev, device_id_type=MESH,
            )

        q_copies = [swap(0, 0, r, r - 1, q_peers[r - 1]) for r in range(1, 4)]
        y_copies = [[swap(which, 0, 2, half, y_peer, half) for half in range(2)] for which in (1, 2)]
        chip_copies = [swap(which, 0, 1, 2, chip_peer) for which in (1, 2)]
        on_copies = [[swap(which, 2, 3, 3 + half, chip_peer, half) for half in range(2)] for which in (1, 2)]

        def pass_on(i):
            for half in range(2):
                y_copies[i][half].wait_recv()
                on_copies[i][half].start()

        wait_for(block(0, 0), a_recv.at[0])
        for copy in q_copies:
            copy.start()

        for which in (1, 2):
            wait_for(block(which, 0), a_recv.at[which])
            for copy in y_copies[which - 1]:
                copy.start()
            chip_copies[which - 1].start()

        wait_for(lists, a_recv.at[3])
        listed = lists[...]
        used[...] = jnp.broadcast_to(jnp.sum(jnp.where(listed >= 0, 1, 0), axis=2, keepdims=True), used.shape)
        listed = jnp.maximum(listed, 0)
        tile_yh = (listed >> 2) & 3
        tile_yl = ((listed >> 1) & 1) ^ jnp.where((tile_yh - yh) % 2 == 0, 1, 0)
        place = (tile_yl ^ yl) * 2 + ((listed & 1) ^ c)
        places[...] = place * SRC + (listed >> 4) * 4 + tile_yh
        to_scalars = pltpu.make_async_copy(places, places_s, list_sem)
        to_scalars.start()

        pass_on(0)
        to_scalars.wait()
        for copy in q_copies + [chip_copies[0]] + on_copies[0]:
            copy.wait_recv()

        pass_on(1)
        for copy in [chip_copies[1]] + on_copies[1]:
            copy.wait_recv()

        lane = lax.broadcasted_iota(jnp.int32, (D, D), 1)
        key_slot = lax.broadcasted_iota(jnp.int32, (1, 256), 1) % D // ROWS
        ones = jnp.ones((256, D), BF16)

        def gathered(which, t, g):
            blocks = [places_s[t, 0, s] for s in range(g * 8, g * 8 + 8)]
            return jnp.concatenate([held[which][b + half * HALF] for half in range(2) for b in blocks], axis=0)

        def weights_of(ts):
            scores = []
            for t in ts:
                limit = jnp.concatenate([used[t], used[t]], axis=1)
                query = jnp.concatenate([q_rows[r * SRC + half * HALF + t] for r in range(4) for half in range(2)], axis=0)
                scores.append([
                    lax.dot_general(query, gathered(1, t, g), (((1,), (1,)), ((), ())), preferred_element_type=F32)
                    + jnp.where(key_slot + g * 8 < limit, 0.0, LOW)
                    for g in range(4)
                ])
            found = []
            stats = stat[ts[0] // 8]
            for t, s in zip(ts, scores):
                top = jnp.maximum(jnp.maximum(s[0], s[1]), jnp.maximum(s[2], s[3]))
                top = jnp.max(top, axis=1, keepdims=True)
                stats = jnp.where(lane == t % 8, top, stats)
                found.append([jnp.exp2((s[g] - top) * SCALE).astype(BF16) for g in range(4)])
            stat[ts[0] // 8] = stats
            return found

        def numerators(ts, found):
            totals = []
            for t, w in zip(ts, found):
                total = jnp.zeros((D, 2 * D), F32)
                for g in range(4):
                    values = jnp.concatenate([gathered(2, t, g), ones], axis=1)
                    total = total + jnp.dot(w[g], values, preferred_element_type=F32)
                totals.append(total)
            stats = stat[ts[0] // 8]
            for t, total in zip(ts, totals):
                stats = jnp.where(lane == t % 8 + 8, total[:, D:], stats)
                numerator = total[:, :D].astype(BF16)
                for r in range(4):
                    for half in range(2):
                        low = r * PART + half * ROWS
                        part[r, half, t] = numerator[low : low + ROWS]
            stat[ts[0] // 8] = stats

        def part_copy(k, r):
            rows = pl.ds(k * PER_CHUNK, PER_CHUNK)
            return pltpu.make_async_remote_copy(
                part.at[r, :, rows], got.at[r - 1, :, rows], d_send.at[k, r - 1], d_recv.at[k, r - 1],
                device_id=q_peers[r - 1], device_id_type=MESH,
            )

        def pair(k):
            return [2 * k, 2 * k + 1]

        def send_parts(k):
            for r in range(1, 4):
                part_copy(k, r).start()

        def chunk(k):
            numerators(pair(k), weights_of(pair(k)))
            send_parts(k)

        stat_copies = [
            [
                pltpu.make_async_remote_copy(
                    packed.at[r, g], got_stat.at[r - 1, g], s_send.at[g, r - 1], s_recv.at[g, r - 1],
                    device_id=q_peers[r - 1], device_id_type=MESH,
                )
                for r in range(1, 4)
            ]
            for g in range(2)
        ]

        def pack(g):
            for r in range(1, 4):
                parts = [stat[g, r * PART + 8 * i : r * PART + 8 * (i + 1), 0:32] for i in range(4)]
                packed[r, g] = jnp.concatenate(parts, axis=1)

        def unpacked(block):
            return jnp.concatenate([block[:, 32 * i : 32 * i + 16] for i in range(4)], axis=0)

        for g in range(2):
            loop(g * 4, g * 4 + 4, chunk)
            pack(g)
            for copy in stat_copies[g]:
                copy.start()

        columns = out_ref.at[:, pl.ds(pl.multiple_of(head * D, D), D)]
        for k in range(CHUNKS):
            if k % 4 == 0:
                g = k // 4
                for copy in stat_copies[g]:
                    copy.wait_recv()
                stats = [stat[g, 0:PART, 0:16]] + [unpacked(got_stat[r, g]) for r in range(3)]
                highest = jnp.maximum(jnp.maximum(stats[0], stats[1]), jnp.maximum(stats[2], stats[3]))
                factors = [jnp.exp2((s - highest) * SCALE) for s in stats]
                denominator = sum(f[:, 0:8] * s[:, 8:16] for f, s in zip(factors, stats))
                factors = [f[:, 0:8] / denominator for f in factors]
            for r in range(1, 4):
                part_copy(k, r).wait_recv()
            for t in pair(k):
                for half in range(2):
                    s = half * HALF + t
                    rows = slice(half * ROWS, (half + 1) * ROWS)
                    terms = [part[0, half, t]] + [got[r, half, t] for r in range(3)]
                    fin[s] = sum(f[rows, t % 8 : t % 8 + 1] * a.astype(F32) for f, a in zip(factors, terms)).astype(BF16)
                    pltpu.make_async_remote_copy(
                        fin.at[s], columns, e_sem.at[0], e_sem.at[1], device_id=source(s), device_id_type=MESH
                    ).start()

        for copy in q_copies + y_copies[0] + y_copies[1] + chip_copies + on_copies[0] + on_copies[1] + stat_copies[0] + stat_copies[1]:
            copy.wait_send()
        for k in range(CHUNKS):
            for r in range(1, 4):
                part_copy(k, r).wait_send()
        wait_for(fin, e_sem.at[0])

    for which in range(3):
        wait_for(rows_in[which], a_send.at[which])
    wait_for(out_ref, e_sem.at[1])

    @pl.when(xh == 0)
    def _():
        wait_for(list_room, a_send.at[3])


def per_device(query, key, value, tile_list):
    dma = pltpu.SemaphoreType.DMA
    return pl.pallas_call(
        kernel,
        out_shape=jax.ShapeDtypeStruct(query.shape, BF16),
        in_specs=[pl.BlockSpec(memory_space=pl.ANY)] * 4,
        out_specs=pl.BlockSpec(memory_space=pl.ANY),
        scratch_shapes=[
            pltpu.VMEM((HEADS, 1, SLOTS), jnp.int32),
            pltpu.VMEM((TILES, 1, SLOTS), jnp.int32),
            pltpu.VMEM((TILES, 1, D), jnp.int32),
            pltpu.VMEM((TILES, 1, SLOTS), jnp.int32),
            pltpu.SMEM((TILES, 1, SLOTS), jnp.int32),
            pltpu.VMEM((4 * SRC, ROWS, D), BF16),
            pltpu.VMEM((4 * SRC, ROWS, D), BF16),
            pltpu.VMEM((4 * SRC, ROWS, D), BF16),
            pltpu.VMEM((4, 2, TILES, ROWS, D), BF16),
            pltpu.VMEM((3, 2, TILES, ROWS, D), BF16),
            pltpu.VMEM((2, D, D), F32),
            pltpu.VMEM((4, 2, 8, D), F32),
            pltpu.VMEM((3, 2, 8, D), F32),
            pltpu.VMEM((SRC, ROWS, D), BF16),
            dma, dma((4,)), dma((4,)), dma((3, 5)), dma((3, 5)),
            dma((CHUNKS, 3)), dma((CHUNKS, 3)), dma((2, 3)), dma((2, 3)), dma((2,)),
        ],
        compiler_params=pltpu.CompilerParams(
            collective_id=0, has_side_effects=True, vmem_limit_bytes=56393728
        ),
        name="attention",
    )(query, key, value, tile_list)


def solution(mesh):
    rows = P(("blk", "uly"), None)
    return jax.shard_map(
        per_device,
        mesh=mesh,
        in_specs=(rows, rows, rows, P("blk", None)),
        out_specs=rows,
        check_vma=False,
    )
```
